256 devices in a mesh: row: 16 (over y, x), col: 16 (over z, core).
Axes of the slice: x: 4, y: 4, z: 8, core: 2. Of those that a mesh axis runs over, the one named last changes fastest.
Arguments:
- rhs: float32 [2048, 256], P('row'), may hold values from -6 to 6
- sep_lower: bfloat16 [2048, 2048], P('row'), may hold values from -0.5 to 0.5
- sep_pattern: int32 [16, 16], replicated, may hold values 0 or 1
- diag_inverse: bfloat16 [2048, 128], replicated, may hold values from -0.5 to 0.5
- child_lower: bfloat16 [2048, 131072], P('row', 'col'), may hold values from -0.0234375 to 0.0234375
- child_ids: int32 [16, 1024], P('row', 'col'), may hold values from 0 to 31
- child_count: int32 [16, 16], P('row', 'col'), may hold values from 1 to 64, 512 in all within a row
- child_x: bfloat16 [65536, 256], P('col'), may hold values from -6 to 6
Outputs:
- solution: bfloat16 [2048, 256], P('row')
The draws below stay inside these ranges and needn't reach their ends.
Inputs may be any that keep to these rules, and one draw needn't show every extreme that they name: `child_count`: for each separator block the counts over the 16 process columns sum to 512, and the largest is exactly 64.
All inputs are finite; a program needn't handle non-finite values.
Results may differ from the reference program's by a relative error of at most 0.02.
Values may be sent and summed in bfloat16 or wider, within the bound.
A program may use at most 64 MiB of HBM per device.

```python
import math
import jax
import jax.numpy as jnp
import numpy as np
from jax import lax

BS = 128
R = 256
LIST = 64
CH_DEV = 32
NSEP = 16
N_COL = 16


def with_ends(drawn, own_key, low, high):
    extent = drawn.shape
    spot = [jax.random.randint(jax.random.fold_in(own_key, axis), (), 0, extent[axis]) for axis in range(len(extent))]
    drawn = drawn.at[tuple(spot)].set(low)
    longest = extent.index(max(extent))
    spot[longest] = (spot[longest] + 1) % extent[longest]
    return drawn.at[tuple(spot)].set(high)


def block_levels(rng, extent, shards, smallest, high):
    def one(dim, blocks):
        draws = jax.random.uniform(jax.random.fold_in(jax.random.fold_in(rng, 6), dim), (blocks,), jnp.float32, smallest / len(shards), high / len(shards))
        return jnp.repeat(jnp.exp(draws), extent[dim] // blocks).reshape((-1,) + (1,) * (len(extent) - dim - 1))

    loudness = one(*shards[0])
    for cut in shards[1:]:
        loudness = loudness * one(*cut)
    return loudness


def length_profile(count, total, reach, slope):
    portions = [(1 << 20) // math.isqrt(standing ** slope) + 1 for standing in range(2, count + 1)]
    spare, given = total - reach - (count - 1), [1] * (count - 1)
    while spare > 0:
        movable = [i for i in range(count - 1) if given[i] < reach]
        mass, left = sum([portions[i] for i in movable]), spare
        for i in movable:
            addition = min(reach - given[i], max(1, left * portions[i] // mass), spare)
            given[i] = given[i] + addition
            spare = spare - addition
    return np.array([reach] + given)


def ragged(key, number_of, total, limit, skew):
    if number_of == 2:
        one = jax.random.randint(key, (), max(1, total - limit), min(limit, total - 1) + 1)
        return jnp.stack([one, total - one])
    sizes = jnp.asarray(length_profile(number_of, total, limit, skew), jnp.int32)
    couples = (number_of - 1) // 2
    donor, sink = sizes[1:1 + 2 * couples:2], sizes[2:2 + 2 * couples:2]
    margin = jnp.minimum(donor - 1, limit - sink)
    passed = jax.random.randint(jax.random.fold_in(key, 1), (couples,), 0, 1 << 20) % (margin + 1)
    sizes = sizes.at[1:1 + 2 * couples:2].set(donor - passed).at[2:2 + 2 * couples:2].set(sink + passed)
    return sizes[jax.random.permutation(jax.random.fold_in(key, 2), number_of)]


def bell_draw(key, dims, scale, reach, split=(), kind=jnp.bfloat16):
    gain = block_levels(key, dims, split, -0.22, 0.18) if split else 1.0
    values = jax.random.normal(key, dims, jnp.float32) * scale * gain
    return jnp.minimum(jnp.maximum(values, -reach), reach).astype(kind)


def setup_inputs(seed: int = 0) -> dict:
    key_list = jax.random.split(jax.random.key(seed), 9)
    rhs = bell_draw(key_list[0], (NSEP * BS, R), 1.0, 6.0, ((0, 16),), jnp.float32)
    sep_lower = bell_draw(key_list[1], (NSEP * BS, NSEP * BS), BS ** -0.5, 0.5, ((0, 16),))
    sep_pattern = with_ends((jax.random.randint(key_list[2], (NSEP, NSEP), 0, 4) < 3).astype(jnp.int32), jax.random.fold_in(key_list[2], 1), 0, 1)
    diag_inverse = bell_draw(key_list[3], (NSEP * BS, BS), BS ** -0.5, 0.5)
    child_lower = bell_draw(key_list[4], (NSEP * BS, N_COL * LIST * BS), (N_COL * LIST * BS // 2) ** -0.5, 0.0234375, ((0, 16), (1, 16)))
    child_ids = with_ends(jax.random.randint(key_list[5], (NSEP, N_COL * LIST), 0, CH_DEV), jax.random.fold_in(key_list[5], 1), 0, CH_DEV - 1).astype(jnp.int32)
    child_count = jax.vmap(lambda own: ragged(own, N_COL, N_COL * LIST // 2, LIST, 2))(jax.random.split(key_list[6], NSEP)).reshape((NSEP, N_COL)).astype(jnp.int32)
    child_x = bell_draw(key_list[7], (N_COL * CH_DEV * BS, R), 1.0, 6.0, ((0, 16),))
    return dict(rhs=rhs, sep_lower=sep_lower, sep_pattern=sep_pattern, diag_inverse=diag_inverse, child_lower=child_lower, child_ids=child_ids, child_count=child_count, child_x=child_x)


def reference(rhs, sep_lower, sep_pattern, diag_inverse, child_lower, child_ids, child_count, child_x):
    blocks_x = child_x.reshape(N_COL * CH_DEV, BS, R)
    slot_range = jnp.arange(LIST, dtype=jnp.int32)
    owners = jnp.arange(N_COL, dtype=jnp.int32)

    def child_term(inputs):
        lower_row, ids_row, count_row = inputs
        chosen = ids_row.reshape(N_COL, LIST) + owners[:, None] * CH_DEV
        live_slots = (slot_range[None, :] < count_row[:, None]).reshape(-1)
        picked = blocks_x[chosen.reshape(-1)]
        picked = jnp.where(live_slots[:, None, None], picked, jnp.zeros((), jnp.bfloat16))
        return jnp.dot(lower_row, picked.reshape(N_COL * LIST * BS, R), preferred_element_type=jnp.float32)

    pending = lax.map(child_term, (child_lower.reshape(NSEP, BS, N_COL * LIST * BS), child_ids, child_count))
    block_rows = jnp.arange(NSEP, dtype=jnp.int32)
    strict_pattern = (sep_pattern * (block_rows[:, None] > block_rows[None, :]).astype(jnp.int32)).astype(jnp.float32)
    solution = []
    for position in range(NSEP):
        residual = (rhs[position * BS:(position + 1) * BS] - pending[position]).astype(jnp.bfloat16)
        solved = jnp.dot(diag_inverse[position * BS:(position + 1) * BS], residual, preferred_element_type=jnp.float32).astype(jnp.bfloat16)
        column = sep_lower[:, position * BS:(position + 1) * BS]
        new_terms = jnp.dot(column, solved, preferred_element_type=jnp.float32).reshape(NSEP, BS, R)
        pending = pending + new_terms * strict_pattern[:, position][:, None, None]
        solution.append(solved)
    return jnp.concatenate(solution, 0)
```

```python
import jax
import jax.numpy as jnp
from jax import lax
from jax.experimental import pallas as pl
from jax.experimental.pallas import tpu as pltpu
from jax.sharding import PartitionSpec as P

MESH = pl.DeviceIdType.MESH
BF16 = jnp.bfloat16
F32 = jnp.float32

ROWS = 16
COLS = 16
CHIPS = COLS // 2
BS = 128
WIDTH = 256
PART = WIDTH // CHIPS
LAST = ROWS - 1
SLOTS = 64
BLOCKS = 32
CHUNKS = 4
VIA = {10: 14}
FAR_FIRST = (4, 3, 5, 2, 6, 1, 7)


def dot_t(a, b):
    return lax.dot_general(a, b, (((1,), (1,)), ((), ())), preferred_element_type=F32)


def kernel(
    pattern, ids, count, rhs_hbm, sep_hbm, dinv_hbm, lower_hbm, x_hbm, out,
    x_all, lower, sep, dinv, rhs, scaled, factor, relay, sums, parts, rhs_t,
    residual, residuals, solved, result,
    load_sem, factor_send, factor_recv, relay_sem, part_send, part_recv,
    residual_send, residual_recv, solved_send, result_send, result_recv,
):
    row, col = lax.axis_index("row"), lax.axis_index("col")
    chip, core = col // 2, lax.rem(col, 2)
    first = core == 0
    solver = first & (row == LAST)

    def other_chip(step):
        return lax.rem(chip + step, CHIPS)

    barrier = pltpu.get_barrier_semaphore()

    def greet(r, c):
        pl.semaphore_signal(barrier, inc=1, device_id=(r, c), device_id_type=MESH)

    for step in FAR_FIRST:
        greet(row, 2 * other_chip(step))

        @pl.when(first)
        def _():
            greet(row, 2 * other_chip(step) + 1)

    greet(row, 2 * chip + 1 - core)

    @pl.when(first & (row != LAST))
    def _():
        greet(LAST, col)

    @pl.when(solver)
    def _():
        for r in range(LAST):
            greet(r, col)

    for a, b in VIA.items():
        @pl.when(first & (row == a))
        def _():
            greet(b, col)

        @pl.when(first & (row == b))
        def _():
            greet(a, col)

    def load(src, dst, sem):
        copy = pltpu.make_async_copy(src, dst, load_sem.at[sem])
        copy.start()
        return copy

    load_sep = load(sep_hbm, sep, 0)
    load_dinv = load(dinv_hbm, dinv, 1)
    load_x = load(x_hbm, x_all.at[pl.ds(0, BLOCKS)], 2)
    span = SLOTS * BS // CHUNKS
    load_lower = [
        load(lower_hbm.at[:, pl.ds(i * span, span)], lower.at[i], 4 + i) for i in range(CHUNKS)
    ]
    load_rhs = load(rhs_hbm, rhs, 3)
    x_all[BLOCKS] = jnp.zeros((BS, WIDTH), BF16)

    load_sep.wait()
    load_dinv.wait()

    @pl.when(first)
    def _():
        own = dinv[pl.ds(pl.multiple_of(row * BS, BS), BS), :]
        for j in range(LAST):
            term = jnp.dot(own, sep[:, j * BS:(j + 1) * BS], preferred_element_type=F32)
            scaled[j] = (term * pattern[row, j].astype(F32)).astype(BF16)

    load_x.wait()
    live = count[0, 0]
    total = jnp.zeros((BS, WIDTH), F32)
    pairs = SLOTS // 2 // CHUNKS
    for i in range(CHUNKS):
        load_lower[i].wait()
        for p in range(pairs):
            j = 2 * (i * pairs + p)
            picked = [x_all[jnp.where(s < live, ids[0, s], BLOCKS)] for s in (j, j + 1)]
            total += jnp.dot(
                lower[i, :, 2 * p * BS:2 * (p + 1) * BS],
                jnp.concatenate(picked, 0),
                preferred_element_type=F32,
            )
    sums[...] = total.T.reshape(CHIPS, PART, BS)
    load_rhs.wait()
    rhs_t[...] = rhs[...].T.reshape(CHIPS, PART, BS)

    via_count = jnp.where((row == 10) | (row == 14), 1, 0)
    pl.semaphore_wait(
        barrier,
        jnp.where(first, COLS - 1 + jnp.where(row == LAST, LAST, 1) + via_count, CHIPS),
    )

    def factor_copy(r):
        via = VIA.get(r)
        if via is None:
            return pltpu.make_async_remote_copy(
                src_ref=scaled.at[pl.ds(0, r)], dst_ref=factor.at[r, pl.ds(0, r)],
                send_sem=factor_send.at[0], recv_sem=factor_recv.at[r],
                device_id=(LAST, col), device_id_type=MESH)
        return pltpu.make_async_remote_copy(
            src_ref=scaled.at[pl.ds(0, r)], dst_ref=relay.at[pl.ds(0, r)],
            send_sem=factor_send.at[0], recv_sem=relay_sem.at[0],
            device_id=(via, col), device_id_type=MESH)

    def relay_copy(r):
        return pltpu.make_async_remote_copy(
            src_ref=relay.at[pl.ds(0, r)], dst_ref=factor.at[r, pl.ds(0, r)],
            send_sem=relay_sem.at[1], recv_sem=factor_recv.at[r],
            device_id=(LAST, col), device_id_type=MESH)

    for r in range(1, LAST):
        @pl.when(first & (row == r))
        def _():
            factor_copy(r).start()

    def part_copy(step):
        to = other_chip(step)
        return pltpu.make_async_remote_copy(
            src_ref=sums.at[to], dst_ref=parts.at[col],
            send_sem=part_send.at[step], recv_sem=part_recv.at[col],
            device_id=(row, 2 * to), device_id_type=MESH)

    for step in FAR_FIRST:
        part_copy(step).start()

    @pl.when(jnp.logical_not(first))
    def _():
        part_copy(0).start()

    def residual_copy():
        return pltpu.make_async_remote_copy(
            src_ref=residual, dst_ref=residuals.at[row],
            send_sem=residual_send.at[0], recv_sem=residual_recv.at[row],
            device_id=(LAST, col), device_id_type=MESH)

    def result_copy(step, to_core):
        return pltpu.make_async_remote_copy(
            src_ref=result.at[chip], dst_ref=result.at[chip],
            send_sem=result_send.at[step, to_core], recv_sem=result_recv.at[chip],
            device_id=(row, 2 * other_chip(step) + to_core), device_id_type=MESH)

    def solved_copy(r):
        return pltpu.make_async_remote_copy(
            src_ref=solved.at[r], dst_ref=result.at[chip],
            send_sem=solved_send.at[r], recv_sem=result_recv.at[chip],
            device_id=(r, col), device_id_type=MESH)

    def result_wait(at):
        pltpu.make_async_remote_copy(
            src_ref=solved.at[0], dst_ref=result.at[at],
            send_sem=result_send.at[0, 0], recv_sem=result_recv.at[at],
            device_id=(row, col), device_id_type=MESH).wait_recv()

    @pl.when(first)
    def _():
        parts[col] = sums[chip]
        for k in range(1, COLS):
            src = lax.rem(col + k, COLS)
            pltpu.make_async_remote_copy(
                src_ref=sums.at[0], dst_ref=parts.at[src],
                send_sem=part_send.at[0], recv_sem=part_recv.at[src],
                device_id=(row, col), device_id_type=MESH).wait_recv()
        summed = parts[0]
        for k in range(1, COLS):
            summed += parts[k]
        value = (rhs_t[chip] - summed).astype(BF16)

        @pl.when(row != LAST)
        def _():
            residual[...] = value
            residual_copy().start()

        @pl.when(row == LAST)
        def _():
            residuals[LAST] = value

    for r, via in VIA.items():
        @pl.when(first & (row == via))
        def _():
            pltpu.make_async_remote_copy(
                src_ref=scaled.at[pl.ds(0, r)], dst_ref=relay.at[pl.ds(0, r)],
                send_sem=factor_send.at[0], recv_sem=relay_sem.at[0],
                device_id=(LAST, col), device_id_type=MESH).wait_recv()
            relay_copy(r).start()

    @pl.when(solver)
    def _():
        done = []
        for r in range(ROWS):
            if r < LAST:
                pltpu.make_async_remote_copy(
                    src_ref=residual, dst_ref=residuals.at[r],
                    send_sem=residual_send.at[0], recv_sem=residual_recv.at[r],
                    device_id=(LAST, col), device_id_type=MESH).wait_recv()
            if 0 < r < LAST:
                pltpu.make_async_remote_copy(
                    src_ref=scaled.at[pl.ds(0, r)], dst_ref=factor.at[r, pl.ds(0, r)],
                    send_sem=factor_send.at[0], recv_sem=factor_recv.at[r],
                    device_id=(LAST, col), device_id_type=MESH).wait_recv()
            block = dot_t(residuals[r], dinv[r * BS:(r + 1) * BS, :])
            if r:
                blocks = [factor[r, j] if r < LAST else scaled[j] for j in range(r)]
                block -= dot_t(jnp.concatenate(done, 1), jnp.concatenate(blocks, 1))
            block = block.astype(BF16)
            done.append(block)
            if r < LAST:
                solved[r] = block
                solved_copy(r).start()
            else:
                result[chip] = block

    @pl.when(first)
    def _():
        @pl.when(row != LAST)
        def _():
            result_wait(chip)

        for step in FAR_FIRST:
            for to_core in range(2):
                result_copy(step, to_core).start()
        result_copy(0, 1).start()

    for step in range(1, CHIPS):
        result_wait(other_chip(step))

    @pl.when(jnp.logical_not(first))
    def _():
        result_wait(chip)

    out[...] = result[...].reshape(WIDTH, BS)

    for r in range(1, LAST):
        @pl.when(first & (row == r))
        def _():
            factor_copy(r).wait_send()
    for r, via in VIA.items():
        @pl.when(first & (row == via))
        def _():
            relay_copy(r).wait_send()
    for step in FAR_FIRST:
        part_copy(step).wait_send()

    @pl.when(jnp.logical_not(first))
    def _():
        part_copy(0).wait_send()

    @pl.when(first)
    def _():
        @pl.when(row != LAST)
        def _():
            residual_copy().wait_send()

        for step in FAR_FIRST:
            for to_core in range(2):
                result_copy(step, to_core).wait_send()
        result_copy(0, 1).wait_send()

    @pl.when(solver)
    def _():
        for r in range(LAST):
            solved_copy(r).wait_send()


def on_device(
    rhs, sep_lower, sep_pattern, diag_inverse, child_lower, child_ids, child_count, child_x
):
    smem = pl.BlockSpec(memory_space=pltpu.SMEM)
    hbm = pl.BlockSpec(memory_space=pl.ANY)
    dma = pltpu.SemaphoreType.DMA
    found = pl.pallas_call(
        kernel,
        out_shape=jax.ShapeDtypeStruct((WIDTH, BS), BF16),
        in_specs=[smem] * 3 + [hbm] * 5,
        out_specs=pl.BlockSpec(memory_space=pltpu.VMEM),
        scratch_shapes=[
            pltpu.VMEM((BLOCKS + 1, BS, WIDTH), BF16),
            pltpu.VMEM((CHUNKS, BS, SLOTS * BS // CHUNKS), BF16),
            pltpu.VMEM((BS, ROWS * BS), BF16),
            pltpu.VMEM((ROWS * BS, BS), BF16),
            pltpu.VMEM((BS, WIDTH), F32),
            pltpu.VMEM((LAST, BS, BS), BF16),
            pltpu.VMEM((LAST, LAST - 1, BS, BS), BF16),
            pltpu.VMEM((10, BS, BS), BF16),
            pltpu.VMEM((CHIPS, PART, BS), F32),
            pltpu.VMEM((COLS, PART, BS), F32),
            pltpu.VMEM((CHIPS, PART, BS), F32),
            pltpu.VMEM((PART, BS), BF16),
            pltpu.VMEM((ROWS, PART, BS), BF16),
            pltpu.VMEM((LAST, PART, BS), BF16),
            pltpu.VMEM((CHIPS, PART, BS), BF16),
            dma((4 + CHUNKS,)),
            dma((1,)),
            dma((ROWS,)),
            dma((2,)),
            dma((CHIPS,)),
            dma((COLS,)),
            dma((1,)),
            dma((ROWS,)),
            dma((ROWS,)),
            dma((CHIPS, 2)),
            dma((CHIPS,)),
        ],
        compiler_params=pltpu.CompilerParams(
            collective_id=0, has_side_effects=True, vmem_limit_bytes=48 * 2**20
        ),
    )(
        sep_pattern, child_ids, child_count, rhs, sep_lower, diag_inverse, child_lower,
        child_x.reshape(BLOCKS, BS, WIDTH),
    )
    return found.T


def solution(mesh):
    in_specs = (
        P("row", None),
        P("row", None),
        P(),
        P(),
        P("row", "col"),
        P("row", "col"),
        P("row", "col"),
        P("col", None),
    )
    return jax.shard_map(
        on_device, mesh=mesh, in_specs=in_specs, out_specs=P("row", None), check_vma=False
    )
```

```python
import jax
import jax.numpy as jnp
from jax import lax
from jax.experimental import pallas as pl
from jax.experimental.pallas import tpu as pltpu
from jax.sharding import PartitionSpec as P

MESH = pl.DeviceIdType.MESH
BF16 = jnp.bfloat16
F32 = jnp.float32

ROWS = 16
COLS = 16
CHIPS = COLS // 2
BS = 128
WIDTH = 256
PART = WIDTH // CHIPS
LAST = ROWS - 1
SLOTS = 64
BLOCKS = 32
CHUNKS = 4
VIA = {10: 14}
FAR_FIRST = (4, 3, 5, 2, 6, 1, 7)


def dot_t(a, b):
    return lax.dot_general(a, b, (((1,), (1,)), ((), ())), preferred_element_type=F32)


def kernel(
    pattern, ids, count, rhs_hbm, sep_hbm, dinv_hbm, lower_hbm, x_hbm, out,
    x_all, lower, sep, dinv, rhs, scaled, factor, relay, sums, parts, rhs_t,
    residual, residuals, solved, result,
    load_sem, factor_send, factor_recv, relay_sem, part_send, part_recv,
    residual_send, residual_recv, solved_send, result_send, result_recv,
):
    row, col = lax.axis_index("row"), lax.axis_index("col")
    chip, core = col // 2, lax.rem(col, 2)
    first = core == 0
    solver = first & (row == LAST)

    def other_chip(step):
        return lax.rem(chip + step, CHIPS)

    barrier = pltpu.get_barrier_semaphore()

    def greet(r, c):
        pl.semaphore_signal(barrier, inc=1, device_id=(r, c), device_id_type=MESH)

    for step in FAR_FIRST:
        greet(row, 2 * other_chip(step))

        @pl.when(first)
        def _():
            greet(row, 2 * other_chip(step) + 1)

    greet(row, 2 * chip + 1 - core)

    @pl.when(first & (row != LAST))
    def _():
        greet(LAST, col)

    @pl.when(solver)
    def _():
        for r in range(LAST):
            greet(r, col)

    for a, b in VIA.items():
        @pl.when(first & (row == a))
        def _():
            greet(b, col)

        @pl.when(first & (row == b))
        def _():
            greet(a, col)

    def load(src, dst, sem):
        copy = pltpu.make_async_copy(src, dst, load_sem.at[sem])
        copy.start()
        return copy

    load_sep = load(sep_hbm, sep, 0)
    load_dinv = load(dinv_hbm, dinv, 1)
    load_x = load(x_hbm, x_all.at[pl.ds(0, BLOCKS)], 2)
    span = SLOTS * BS // CHUNKS
    load_lower = [
        load(lower_hbm.at[:, pl.ds(i * span, span)], lower.at[i], 4 + i) for i in range(CHUNKS)
    ]
    load_rhs = load(rhs_hbm, rhs, 3)
    x_all[BLOCKS] = jnp.zeros((BS, WIDTH), BF16)

    load_sep.wait()
    load_dinv.wait()

    @pl.when(first)
    def _():
        own = dinv[pl.ds(pl.multiple_of(row * BS, BS), BS), :]
        for j in range(LAST):
            term = jnp.dot(own, sep[:, j * BS:(j + 1) * BS], preferred_element_type=F32)
            scaled[j] = (term * pattern[row, j].astype(F32)).astype(BF16)

    load_x.wait()
    live = count[0, 0]
    total = jnp.zeros((BS, WIDTH), F32)
    pairs = SLOTS // 2 // CHUNKS
    for i in range(CHUNKS):
        load_lower[i].wait()
        for p in range(pairs):
            j = 2 * (i * pairs + p)
            picked = [x_all[jnp.where(s < live, ids[0, s], BLOCKS)] for s in (j, j + 1)]
            total += jnp.dot(
                lower[i, :, 2 * p * BS:2 * (p + 1) * BS],
                jnp.concatenate(picked, 0),
                preferred_element_type=F32,
            )
    sums[...] = total.T.reshape(CHIPS, PART, BS)
    load_rhs.wait()
    rhs_t[...] = rhs[...].T.reshape(CHIPS, PART, BS)

    via_count = jnp.where((row == 10) | (row == 14), 1, 0)
    pl.semaphore_wait(
        barrier,
        jnp.where(first, COLS - 1 + jnp.where(row == LAST, LAST, 1) + via_count, CHIPS),
    )

    def factor_copy(r):
        via = VIA.get(r)
        if via is None:
            return pltpu.make_async_remote_copy(
                src_ref=scaled.at[pl.ds(0, r)], dst_ref=factor.at[r, pl.ds(0, r)],
                send_sem=factor_send.at[0], recv_sem=factor_recv.at[r],
                device_id=(LAST, col), device_id_type=MESH)
        return pltpu.make_async_remote_copy(
            src_ref=scaled.at[pl.ds(0, r)], dst_ref=relay.at[pl.ds(0, r)],
            send_sem=factor_send.at[0], recv_sem=relay_sem.at[0],
            device_id=(via, col), device_id_type=MESH)

    def relay_copy(r):
        return pltpu.make_async_remote_copy(
            src_ref=relay.at[pl.ds(0, r)], dst_ref=factor.at[r, pl.ds(0, r)],
            send_sem=relay_sem.at[1], recv_sem=factor_recv.at[r],
            device_id=(LAST, col), device_id_type=MESH)

    for r in range(1, LAST):
        @pl.when(first & (row == r))
        def _():
            factor_copy(r).start()

    def part_copy(step):
        to = other_chip(step)
        return pltpu.make_async_remote_copy(
            src_ref=sums.at[to], dst_ref=parts.at[col],
            send_sem=part_send.at[step], recv_sem=part_recv.at[col],
            device_id=(row, 2 * to), device_id_type=MESH)

    for step in FAR_FIRST:
        part_copy(step).start()

    @pl.when(jnp.logical_not(first))
    def _():
        part_copy(0).start()

    def residual_copy():
        return pltpu.make_async_remote_copy(
            src_ref=residual, dst_ref=residuals.at[row],
            send_sem=residual_send.at[0], recv_sem=residual_recv.at[row],
            device_id=(LAST, col), device_id_type=MESH)

    def result_copy(step, to_core):
        return pltpu.make_async_remote_copy(
            src_ref=result.at[chip], dst_ref=result.at[chip],
            send_sem=result_send.at[step, to_core], recv_sem=result_recv.at[chip],
            device_id=(row, 2 * other_chip(step) + to_core), device_id_type=MESH)

    def solved_copy(r):
        return pltpu.make_async_remote_copy(
            src_ref=solved.at[r], dst_ref=result.at[chip],
            send_sem=solved_send.at[r], recv_sem=result_recv.at[chip],
            device_id=(r, col), device_id_type=MESH)

    def result_wait(at):
        pltpu.make_async_remote_copy(
            src_ref=solved.at[0], dst_ref=result.at[at],
            send_sem=result_send.at[0, 0], recv_sem=result_recv.at[at],
            device_id=(row, col), device_id_type=MESH).wait_recv()

    @pl.when(first)
    def _():
        parts[col] = sums[chip]
        for k in range(1, COLS):
            src = lax.rem(col + k, COLS)
            pltpu.make_async_remote_copy(
                src_ref=sums.at[0], dst_ref=parts.at[src],
                send_sem=part_send.at[0], recv_sem=part_recv.at[src],
                device_id=(row, col), device_id_type=MESH).wait_recv()
        summed = parts[0]
        for k in range(1, COLS):
            summed += parts[k]
        value = (rhs_t[chip] - summed).astype(BF16)

        @pl.when(row != LAST)
        def _():
            residual[...] = value
            residual_copy().start()

        @pl.when(row == LAST)
        def _():
            residuals[LAST] = value

    for r, via in VIA.items():
        @pl.when(first & (row == via))
        def _():
            pltpu.make_async_remote_copy(
                src_ref=scaled.at[pl.ds(0, r)], dst_ref=relay.at[pl.ds(0, r)],
                send_sem=factor_send.at[0], recv_sem=relay_sem.at[0],
                device_id=(LAST, col), device_id_type=MESH).wait_recv()
            relay_copy(r).start()

    @pl.when(solver)
    def _():
        done = []
        for r in range(ROWS):
            if r < LAST:
                pltpu.make_async_remote_copy(
                    src_ref=residual, dst_ref=residuals.at[r],
                    send_sem=residual_send.at[0], recv_sem=residual_recv.at[r],
                    device_id=(LAST, col), device_id_type=MESH).wait_recv()
            if 0 < r < LAST:
                pltpu.make_async_remote_copy(
                    src_ref=scaled.at[pl.ds(0, r)], dst_ref=factor.at[r, pl.ds(0, r)],
                    send_sem=factor_send.at[0], recv_sem=factor_recv.at[r],
                    device_id=(LAST, col), device_id_type=MESH).wait_recv()
            block = dot_t(residuals[r], dinv[r * BS:(r + 1) * BS, :])
            if r:
                blocks = [factor[r, j] if r < LAST else scaled[j] for j in range(r)]
                block -= dot_t(jnp.concatenate(done, 1), jnp.concatenate(blocks, 1))
            block = block.astype(BF16)
            done.append(block)
            if r < LAST:
                solved[r] = block
                solved_copy(r).start()
            else:
                result[chip] = block

    @pl.when(first)
    def _():
        @pl.when(row != LAST)
        def _():
            result_wait(chip)

        for step in FAR_FIRST:
            for to_core in range(2):
                result_copy(step, to_core).start()
        result_copy(0, 1).start()

    for step in range(1, CHIPS):
        result_wait(other_chip(step))

    @pl.when(jnp.logical_not(first))
    def _():
        result_wait(chip)

    out[...] = result[...].reshape(WIDTH, BS)

    for r in range(1, LAST):
        @pl.when(first & (row == r))
        def _():
            factor_copy(r).wait_send()
    for r, via in VIA.items():
        @pl.when(first & (row == via))
        def _():
            relay_copy(r).wait_send()
    for step in FAR_FIRST:
        part_copy(step).wait_send()

    @pl.when(jnp.logical_not(first))
    def _():
        part_copy(0).wait_send()

    @pl.when(first)
    def _():
        @pl.when(row != LAST)
        def _():
            residual_copy().wait_send()

        for step in FAR_FIRST:
            for to_core in range(2):
                result_copy(step, to_core).wait_send()
        result_copy(0, 1).wait_send()

    @pl.when(solver)
    def _():
        for r in range(LAST):
            solved_copy(r).wait_send()


def on_device(
    rhs, sep_lower, sep_pattern, diag_inverse, child_lower, child_ids, child_count, child_x
):
    smem = pl.BlockSpec(memory_space=pltpu.SMEM)
    hbm = pl.BlockSpec(memory_space=pltpu.HBM)
    dma = pltpu.SemaphoreType.DMA
    found = pl.pallas_call(
        kernel,
        out_shape=jax.ShapeDtypeStruct((WIDTH, BS), BF16),
        in_specs=[smem] * 3 + [hbm] * 5,
        out_specs=pl.BlockSpec(memory_space=pltpu.VMEM),
        scratch_shapes=[
            pltpu.VMEM((BLOCKS + 1, BS, WIDTH), BF16),
            pltpu.VMEM((CHUNKS, BS, SLOTS * BS // CHUNKS), BF16),
            pltpu.VMEM((BS, ROWS * BS), BF16),
            pltpu.VMEM((ROWS * BS, BS), BF16),
            pltpu.VMEM((BS, WIDTH), F32),
            pltpu.VMEM((LAST, BS, BS), BF16),
            pltpu.VMEM((LAST, LAST - 1, BS, BS), BF16),
            pltpu.VMEM((10, BS, BS), BF16),
            pltpu.VMEM((CHIPS, PART, BS), F32),
            pltpu.VMEM((COLS, PART, BS), F32),
            pltpu.VMEM((CHIPS, PART, BS), F32),
            pltpu.VMEM((PART, BS), BF16),
            pltpu.VMEM((ROWS, PART, BS), BF16),
            pltpu.VMEM((LAST, PART, BS), BF16),
            pltpu.VMEM((CHIPS, PART, BS), BF16),
            dma((4 + CHUNKS,)),
            dma((1,)),
            dma((ROWS,)),
            dma((2,)),
            dma((CHIPS,)),
            dma((COLS,)),
            dma((1,)),
            dma((ROWS,)),
            dma((ROWS,)),
            dma((CHIPS, 2)),
            dma((CHIPS,)),
        ],
        compiler_params=pltpu.CompilerParams(
            collective_id=0, has_side_effects=True, vmem_limit_bytes=60 * 2**20
        ),
    )(
        sep_pattern, child_ids, child_count, rhs, sep_lower, diag_inverse, child_lower,
        child_x.reshape(BLOCKS, BS, WIDTH),
    )
    return found.T


def solution(mesh):
    in_specs = (
        P("row", None),
        P("row", None),
        P(),
        P(),
        P("row", "col"),
        P("row", "col"),
        P("row", "col"),
        P("col", None),
    )
    return jax.shard_map(
        on_device, mesh=mesh, in_specs=in_specs, out_specs=P("row", None), check_vma=False
    )
```

```python
import jax
import jax.numpy as jnp
from jax import lax
from jax.experimental import pallas as pl
from jax.experimental.pallas import tpu as pltpu
from jax.sharding import PartitionSpec as P

MESH = pl.DeviceIdType.MESH
BF16 = jnp.bfloat16
F32 = jnp.float32

ROWS = 16
COLS = 16
CHIPS = COLS // 2
BS = 128
WIDTH = 256
PART = WIDTH // CHIPS
LAST = ROWS - 1
SLOTS = 64
BLOCKS = 32
CHUNKS = 4
VIA = {10: 14}
FAR_FIRST = (4, 3, 5, 2, 6, 1, 7)


def dot_t(a, b):
    return lax.dot_general(a, b, (((1,), (1,)), ((), ())), preferred_element_type=F32)


def kernel(
    pattern_hbm, ids_hbm, count_hbm, rhs_hbm, sep_hbm, dinv_hbm, lower_hbm, x_hbm, out,
    pattern, ids, count, x_all, lower, sep, dinv, rhs, scaled, factor, relay, sums, parts, base,
    residual, residuals, solved, result,
    load_sem, factor_send, factor_recv, relay_sem, part_send, part_recv,
    residual_send, residual_recv, solved_send, result_send, result_recv,
):
    row, col = lax.axis_index("row"), lax.axis_index("col")
    chip, core = col // 2, lax.rem(col, 2)
    first = core == 0
    solver = first & (row == LAST)

    def other_chip(step):
        return lax.rem(chip + step, CHIPS)

    barrier = pltpu.get_barrier_semaphore()

    def greet(r, c):
        pl.semaphore_signal(barrier, inc=1, device_id=(r, c), device_id_type=MESH)

    for step in FAR_FIRST:
        greet(row, 2 * other_chip(step))
        greet(row, 2 * other_chip(step) + 1)

    greet(row, 2 * chip + 1 - core)

    @pl.when(row != LAST)
    def _():
        greet(LAST, 2 * chip)

    @pl.when(solver)
    def _():
        for r in range(LAST):
            greet(r, col)

    for a, b in VIA.items():
        @pl.when(first & (row == a))
        def _():
            greet(b, col)

        @pl.when(first & (row == b))
        def _():
            greet(a, col)

    def load(src, dst, sem):
        copy = pltpu.make_async_copy(src, dst, load_sem.at[sem])
        copy.start()
        return copy

    load_sep = load(sep_hbm, sep, 0)
    load_small = [
        load(src, dst, 4 + i)
        for i, (src, dst) in enumerate([(pattern_hbm, pattern), (ids_hbm, ids), (count_hbm, count)])
    ]
    load_dinv = load(dinv_hbm, dinv, 1)
    load_x = load(x_hbm, x_all.at[pl.ds(0, BLOCKS)], 2)
    span = SLOTS * BS // CHUNKS
    load_lower = [
        load(lower_hbm.at[:, pl.ds(i * span, span)], lower.at[i], 7 + i) for i in range(CHUNKS)
    ]
    load_rhs = load(rhs_hbm, rhs, 3)
    x_all[BLOCKS] = jnp.zeros((BS, WIDTH), BF16)

    for copy in load_small:
        copy.wait()
    load_sep.wait()
    load_dinv.wait()

    @pl.when(first)
    def _():
        own = dinv[pl.ds(pl.multiple_of(row * BS, BS), BS), :]
        for j in range(LAST):
            term = jnp.dot(own, sep[:, j * BS:(j + 1) * BS], preferred_element_type=F32)
            scaled[j] = (term * pattern[row, j].astype(F32)).astype(BF16)

    load_x.wait()
    live = count[0, 0]
    total = jnp.zeros((BS, WIDTH), F32)
    pairs = SLOTS // 2 // CHUNKS
    for i in range(CHUNKS):
        load_lower[i].wait()
        for p in range(pairs):
            j = 2 * (i * pairs + p)
            picked = [x_all[jnp.where(s < live, ids[0, s], BLOCKS)] for s in (j, j + 1)]
            total += jnp.dot(
                lower[i, :, 2 * p * BS:2 * (p + 1) * BS],
                jnp.concatenate(picked, 0),
                preferred_element_type=F32,
            )
    sums[...] = total.T.reshape(CHIPS, PART, BS).astype(BF16)
    load_rhs.wait()
    base[...] = (rhs[...] - total).T.reshape(CHIPS, PART, BS)

    via_count = jnp.where((row == 10) | (row == 14), 1, 0)
    pl.semaphore_wait(
        barrier,
        COLS - 1 + jnp.where(first, jnp.where(row == LAST, 2 * LAST, 1) + via_count, 0),
    )

    def factor_copy(r):
        via = VIA.get(r)
        if via is None:
            return pltpu.make_async_remote_copy(
                src_ref=scaled.at[pl.ds(0, r)], dst_ref=factor.at[r, pl.ds(0, r)],
                send_sem=factor_send.at[0], recv_sem=factor_recv.at[r],
                device_id=(LAST, col), device_id_type=MESH)
        return pltpu.make_async_remote_copy(
            src_ref=scaled.at[pl.ds(0, r)], dst_ref=relay.at[pl.ds(0, r)],
            send_sem=factor_send.at[0], recv_sem=relay_sem.at[0],
            device_id=(via, col), device_id_type=MESH)

    def relay_copy(r):
        return pltpu.make_async_remote_copy(
            src_ref=relay.at[pl.ds(0, r)], dst_ref=factor.at[r, pl.ds(0, r)],
            send_sem=relay_sem.at[1], recv_sem=factor_recv.at[r],
            device_id=(LAST, col), device_id_type=MESH)

    for r in range(1, LAST):
        @pl.when(first & (row == r))
        def _():
            factor_copy(r).start()

    def part_copy(step):
        to = other_chip(step)
        return pltpu.make_async_remote_copy(
            src_ref=sums.at[to], dst_ref=parts.at[col],
            send_sem=part_send.at[step], recv_sem=part_recv.at[col],
            device_id=(row, 2 * to), device_id_type=MESH)

    for step in FAR_FIRST:
        part_copy(step).start()

    @pl.when(jnp.logical_not(first))
    def _():
        part_copy(0).start()

    def residual_copy():
        return pltpu.make_async_remote_copy(
            src_ref=residual, dst_ref=residuals.at[row],
            send_sem=residual_send.at[0], recv_sem=residual_recv.at[row],
            device_id=(LAST, col), device_id_type=MESH)

    def result_copy(step):
        return pltpu.make_async_remote_copy(
            src_ref=result.at[chip], dst_ref=result.at[chip],
            send_sem=result_send.at[step], recv_sem=result_recv.at[chip],
            device_id=(row, 2 * other_chip(step) + core), device_id_type=MESH)

    def solved_copy(r, to_core):
        return pltpu.make_async_remote_copy(
            src_ref=solved.at[r], dst_ref=result.at[chip],
            send_sem=solved_send.at[r, to_core], recv_sem=result_recv.at[chip],
            device_id=(r, 2 * chip + to_core), device_id_type=MESH)

    def result_wait(at):
        pltpu.make_async_remote_copy(
            src_ref=solved.at[0], dst_ref=result.at[at],
            send_sem=result_send.at[0], recv_sem=result_recv.at[at],
            device_id=(row, col), device_id_type=MESH).wait_recv()

    @pl.when(first)
    def _():
        parts[col] = jnp.zeros((PART, BS), BF16)
        for k in range(1, COLS):
            src = lax.rem(col + k, COLS)
            pltpu.make_async_remote_copy(
                src_ref=sums.at[0], dst_ref=parts.at[src],
                send_sem=part_send.at[0], recv_sem=part_recv.at[src],
                device_id=(row, col), device_id_type=MESH).wait_recv()
        value = base[chip]
        for k in range(COLS):
            value -= parts[k].astype(F32)
        value = value.astype(BF16)

        @pl.when(row != LAST)
        def _():
            residual[...] = value
            residual_copy().start()

        @pl.when(row == LAST)
        def _():
            residuals[LAST] = value

    for r, via in VIA.items():
        @pl.when(first & (row == via))
        def _():
            pltpu.make_async_remote_copy(
                src_ref=scaled.at[pl.ds(0, r)], dst_ref=relay.at[pl.ds(0, r)],
                send_sem=factor_send.at[0], recv_sem=relay_sem.at[0],
                device_id=(LAST, col), device_id_type=MESH).wait_recv()
            relay_copy(r).start()

    @pl.when(solver)
    def _():
        for r in range(LAST):
            pltpu.make_async_remote_copy(
                src_ref=residual, dst_ref=residuals.at[r],
                send_sem=residual_send.at[0], recv_sem=residual_recv.at[r],
                device_id=(LAST, col), device_id_type=MESH).wait_recv()
        start = [dot_t(residuals[r], dinv[r * BS:(r + 1) * BS, :]) for r in range(ROWS)]
        for r in range(1, LAST):
            pltpu.make_async_remote_copy(
                src_ref=scaled.at[pl.ds(0, r)], dst_ref=factor.at[r, pl.ds(0, r)],
                send_sem=factor_send.at[0], recv_sem=factor_recv.at[r],
                device_id=(LAST, col), device_id_type=MESH).wait_recv()
        done = []
        for r in range(ROWS):
            block = start[r]
            blocks = [factor[r, j] if r < LAST else scaled[j] for j in range(r)]
            if r > 1:
                block -= dot_t(jnp.concatenate(done[:-1], 1), jnp.concatenate(blocks[:-1], 1))
            if r:
                block -= dot_t(done[-1], blocks[-1])
            block = block.astype(BF16)
            done.append(block)
            solved[r] = block
            if r < LAST:
                for to_core in range(2):
                    solved_copy(r, to_core).start()
            else:
                solved_copy(r, 1).start()
                result[chip] = block

    @pl.when(jnp.logical_not(solver))
    def _():
        result_wait(chip)

    for step in FAR_FIRST:
        result_copy(step).start()
    for step in range(1, CHIPS):
        result_wait(other_chip(step))

    out[...] = result[...].reshape(WIDTH, BS)

    for r in range(1, LAST):
        @pl.when(first & (row == r))
        def _():
            factor_copy(r).wait_send()
    for r, via in VIA.items():
        @pl.when(first & (row == via))
        def _():
            relay_copy(r).wait_send()
    for step in FAR_FIRST:
        part_copy(step).wait_send()
        result_copy(step).wait_send()

    @pl.when(jnp.logical_not(first))
    def _():
        part_copy(0).wait_send()

    @pl.when(first & (row != LAST))
    def _():
        residual_copy().wait_send()

    @pl.when(solver)
    def _():
        for r in range(ROWS):
            for to_core in range(2):
                if r < LAST or to_core:
                    solved_copy(r, to_core).wait_send()


def on_device(
    rhs, sep_lower, sep_pattern, diag_inverse, child_lower, child_ids, child_count, child_x
):
    hbm = pl.BlockSpec(memory_space=pltpu.HBM)
    dma = pltpu.SemaphoreType.DMA
    found = pl.pallas_call(
        kernel,
        out_shape=pltpu.VMEM((WIDTH, BS), BF16),
        in_specs=[hbm] * 8,
        out_specs=pl.BlockSpec(memory_space=pltpu.VMEM),
        scratch_shapes=[
            pltpu.SMEM((ROWS, ROWS), jnp.int32),
            pltpu.SMEM((1, SLOTS), jnp.int32),
            pltpu.SMEM((1, 1), jnp.int32),
            pltpu.VMEM((BLOCKS + 1, BS, WIDTH), BF16),
            pltpu.VMEM((CHUNKS, BS, SLOTS * BS // CHUNKS), BF16),
            pltpu.VMEM((BS, ROWS * BS), BF16),
            pltpu.VMEM((ROWS * BS, BS), BF16),
            pltpu.VMEM((BS, WIDTH), F32),
            pltpu.VMEM((LAST, BS, BS), BF16),
            pltpu.VMEM((LAST, LAST - 1, BS, BS), BF16),
            pltpu.VMEM((10, BS, BS), BF16),
            pltpu.VMEM((CHIPS, PART, BS), BF16),
            pltpu.VMEM((COLS, PART, BS), BF16),
            pltpu.VMEM((CHIPS, PART, BS), F32),
            pltpu.VMEM((PART, BS), BF16),
            pltpu.VMEM((ROWS, PART, BS), BF16),
            pltpu.VMEM((ROWS, PART, BS), BF16),
            pltpu.VMEM((CHIPS, PART, BS), BF16),
            dma((7 + CHUNKS,)),
            dma((1,)),
            dma((ROWS,)),
            dma((2,)),
            dma((CHIPS,)),
            dma((COLS,)),
            dma((1,)),
            dma((ROWS,)),
            dma((ROWS, 2)),
            dma((CHIPS,)),
            dma((CHIPS,)),
        ],
        compiler_params=pltpu.CompilerParams(
            collective_id=0, has_side_effects=True, vmem_limit_bytes=60 * 2**20
        ),
    )(
        sep_pattern, child_ids, child_count, rhs, sep_lower, diag_inverse, child_lower,
        child_x.reshape(BLOCKS, BS, WIDTH),
    )
    return found.T


def solution(mesh):
    in_specs = (
        P("row", None),
        P("row", None),
        P(),
        P(),
        P("row", "col"),
        P("row", "col"),
        P("row", "col"),
        P("col", None),
    )
    return jax.shard_map(
        on_device, mesh=mesh, in_specs=in_specs, out_specs=P("row", None), check_vma=False
    )
```

```python
import jax
import jax.numpy as jnp
from jax import lax
from jax.experimental import pallas as pl
from jax.experimental.pallas import tpu as pltpu
from jax.sharding import PartitionSpec as P

MESH = pl.DeviceIdType.MESH
BF16 = jnp.bfloat16
F32 = jnp.float32

ROWS = 16
COLS = 16
CHIPS = COLS // 2
SOLVERS = CHIPS // 2
BS = 128
WIDTH = 256
PART = WIDTH // SOLVERS
LAST = ROWS - 1
SLOTS = 64
BLOCKS = 32
CHUNKS = 4
FAR_FIRST = (4, 3, 5, 2, 6, 1, 7)

VIA = {12: [(4, 0, 4, 0), (5, 0, 5, 4)], 14: [(10, 0, 5, 0), (10, 5, 10, 5)]}
UP = [(11, 0, 4, 0), (11, 4, 8, 4), (11, 8, 11, 8)]
DOWN = [(12, 0, 4, 11), (12, 4, 8, 15), (12, 8, 12, 19)]
SIDE = sorted({piece[0] for piece in UP + DOWN})
ROUTED = {piece[0] for pieces in VIA.values() for piece in pieces} | set(SIDE)
STRAIGHT = [(r, 0, r, 0) for r in range(1, LAST) if r not in ROUTED]
PIECES = STRAIGHT + [piece for pieces in VIA.values() for piece in pieces] + UP + DOWN
RELAY_BLOCKS = 23


def dot_t(a, b):
    return lax.dot_general(a, b, (((1,), (1,)), ((), ())), preferred_element_type=F32)


def any_of(value, options):
    found = value == options[0]
    for option in options[1:]:
        found = found | (value == option)
    return found


def kernel(
    pattern_hbm, ids_hbm, count_hbm, rhs_hbm, sep_hbm, dinv_hbm, lower_hbm, x_hbm, out,
    pattern, ids, count, x_all, lower, sep, dinv, rhs, scaled, factor, relay, sums, parts, base,
    residual, residuals, solved, result,
    load_sem, factor_send, factor_recv, relay_send, relay_recv, part_send, part_recv,
    residual_send, residual_recv, solved_send, result_send, result_recv,
):
    row, col = lax.axis_index("row"), lax.axis_index("col")
    chip, core = col // 2, lax.rem(col, 2)
    mine = chip // 2
    even = lax.rem(chip, 2) == 0
    first = core == 0
    owner = first & even
    helper = even & (core == 1)
    solver = owner & (row == LAST)
    side = first & jnp.logical_not(even)

    def other_chip(step):
        return lax.rem(chip + step, CHIPS)

    barrier = pltpu.get_barrier_semaphore()

    def greet(r, c):
        pl.semaphore_signal(barrier, inc=1, device_id=(r, c), device_id_type=MESH)

    for step in FAR_FIRST:
        greet(row, 2 * other_chip(step))
        greet(row, 2 * other_chip(step) + 1)
    greet(row, 2 * chip + 1 - core)

    @pl.when(even & (row != LAST))
    def _():
        greet(LAST, 2 * chip)

    @pl.when(solver)
    def _():
        for r in range(LAST):
            greet(r, col)
        for via in VIA:
            greet(via, 2 * chip + 1)

    @pl.when(side & (row == LAST))
    def _():
        for r in SIDE:
            greet(r, col)

    for via, pieces in VIA.items():
        @pl.when(helper & (row == via))
        def _():
            for r in sorted({piece[0] for piece in pieces}):
                greet(r, 2 * chip)

    def load(src, dst, sem):
        copy = pltpu.make_async_copy(src, dst, load_sem.at[sem])
        copy.start()
        return copy

    load_sep = load(sep_hbm, sep, 0)
    load_dinv = load(dinv_hbm, dinv, 1)
    load_x = load(x_hbm, x_all.at[pl.ds(0, BLOCKS)], 2)
    load_small = [
        load(src, dst, 4 + i)
        for i, (src, dst) in enumerate([(pattern_hbm, pattern), (ids_hbm, ids), (count_hbm, count)])
    ]
    span = SLOTS * BS // CHUNKS
    load_lower = [
        load(lower_hbm.at[:, pl.ds(i * span, span)], lower.at[i], 7 + i) for i in range(CHUNKS)
    ]
    load_rhs = load(rhs_hbm, rhs, 3)
    x_all[BLOCKS] = jnp.zeros((BS, WIDTH), BF16)
    for copy in load_small:
        copy.wait()

    load_sep.wait()
    load_dinv.wait()

    @pl.when(first)
    def _():
        own = dinv[pl.ds(pl.multiple_of(row * BS, BS), BS), :]
        for j in range(LAST):
            term = jnp.dot(own, sep[:, j * BS:(j + 1) * BS], preferred_element_type=F32)
            scaled[j] = (term * pattern[row, j].astype(F32)).astype(BF16)

    load_x.wait()
    live = count[0, 0]
    total = jnp.zeros((BS, WIDTH), F32)
    pairs = SLOTS // 2 // CHUNKS
    for i in range(CHUNKS):
        load_lower[i].wait()
        for p in range(pairs):
            j = 2 * (i * pairs + p)
            picked = [x_all[jnp.where(s < live, ids[0, s], BLOCKS)] for s in (j, j + 1)]
            total += jnp.dot(
                lower[i, :, 2 * p * BS:2 * (p + 1) * BS],
                jnp.concatenate(picked, 0),
                preferred_element_type=F32,
            )
    sums[...] = total.T.reshape(SOLVERS, PART, BS).astype(BF16)
    load_rhs.wait()
    base[...] = (rhs[...] - total).T.reshape(SOLVERS, PART, BS)

    plane = jnp.where(row == LAST, 2 * LAST, 1)
    for via, pieces in VIA.items():
        plane += jnp.where(any_of(row, sorted({piece[0] for piece in pieces})), 1, 0)
    greeted = jnp.where(owner, plane, 0) + jnp.where(side & any_of(row, SIDE), 1, 0)
    greeted += jnp.where(helper & any_of(row, list(VIA)), 1, 0)
    pl.semaphore_wait(barrier, COLS - 1 + greeted)

    def straight_copy(piece):
        r, lo, hi, _ = piece
        i = PIECES.index(piece)
        return pltpu.make_async_remote_copy(
            src_ref=scaled.at[pl.ds(lo, hi - lo)], dst_ref=factor.at[r, pl.ds(lo, hi - lo)],
            send_sem=factor_send.at[i], recv_sem=factor_recv.at[i],
            device_id=(LAST, col), device_id_type=MESH)

    def first_leg(piece, via, to_core=0):
        _, lo, hi, at = piece
        i = PIECES.index(piece)
        return pltpu.make_async_remote_copy(
            src_ref=scaled.at[pl.ds(lo, hi - lo)], dst_ref=relay.at[pl.ds(at, hi - lo)],
            send_sem=factor_send.at[i], recv_sem=relay_recv.at[i],
            device_id=(via, 2 * chip + to_core), device_id_type=MESH)

    def second_leg(piece, to):
        r, lo, hi, at = piece
        i = PIECES.index(piece)
        return pltpu.make_async_remote_copy(
            src_ref=relay.at[pl.ds(at, hi - lo)], dst_ref=factor.at[r, pl.ds(lo, hi - lo)],
            send_sem=relay_send.at[i], recv_sem=factor_recv.at[i],
            device_id=(LAST, 2 * other_chip(to)), device_id_type=MESH)

    def pass_on(piece, to):
        first_leg(piece, LAST).wait_recv()
        second_leg(piece, to).start()

    for piece in STRAIGHT:
        @pl.when(owner & (row == piece[0]))
        def _():
            straight_copy(piece).start()

    for via, pieces in VIA.items():
        for piece in pieces:
            @pl.when(owner & (row == piece[0]))
            def _():
                first_leg(piece, via, 1).start()

    for piece in UP + DOWN:
        @pl.when(side & (row == piece[0]))
        def _():
            first_leg(piece, LAST).start()

    def part_copy(step):
        to = lax.rem(mine + step, SOLVERS)
        return pltpu.make_async_remote_copy(
            src_ref=sums.at[to], dst_ref=parts.at[col],
            send_sem=part_send.at[step], recv_sem=part_recv.at[col],
            device_id=(row, 4 * to), device_id_type=MESH)

    for step in (2, 3, 1):
        part_copy(step).start()

    @pl.when(jnp.logical_not(owner))
    def _():
        part_copy(0).start()

    def residual_copy():
        return pltpu.make_async_remote_copy(
            src_ref=residual, dst_ref=residuals.at[row],
            send_sem=residual_send.at[0], recv_sem=residual_recv.at[row],
            device_id=(LAST, col), device_id_type=MESH)

    def result_copy(step):
        return pltpu.make_async_remote_copy(
            src_ref=result.at[mine], dst_ref=result.at[mine],
            send_sem=result_send.at[step], recv_sem=result_recv.at[mine],
            device_id=(row, 2 * other_chip(step) + core), device_id_type=MESH)

    def solved_copy(r, to_core):
        return pltpu.make_async_remote_copy(
            src_ref=solved.at[r], dst_ref=result.at[mine],
            send_sem=solved_send.at[r, to_core], recv_sem=result_recv.at[mine],
            device_id=(r, 2 * chip + to_core), device_id_type=MESH)

    def result_wait(at):
        pltpu.make_async_remote_copy(
            src_ref=solved.at[0], dst_ref=result.at[at],
            send_sem=result_send.at[0], recv_sem=result_recv.at[at],
            device_id=(row, col), device_id_type=MESH).wait_recv()

    @pl.when(side & (row == LAST))
    def _():
        for up, down in zip(UP, DOWN):
            pass_on(up, CHIPS - 1)
            pass_on(down, 1)

    for via, pieces in VIA.items():
        @pl.when(helper & (row == via))
        def _():
            for piece in pieces:
                pass_on(piece, 0)

    @pl.when(owner)
    def _():
        parts[col] = jnp.zeros((PART, BS), BF16)
        for k in range(1, COLS):
            src = lax.rem(col + k, COLS)
            pltpu.make_async_remote_copy(
                src_ref=sums.at[0], dst_ref=parts.at[src],
                send_sem=part_send.at[0], recv_sem=part_recv.at[src],
                device_id=(row, col), device_id_type=MESH).wait_recv()
        value = base[mine]
        for k in range(COLS):
            value -= parts[k].astype(F32)
        value = value.astype(BF16)

        @pl.when(row != LAST)
        def _():
            residual[...] = value
            residual_copy().start()

        @pl.when(row == LAST)
        def _():
            residuals[LAST] = value

    @pl.when(solver)
    def _():
        for r in range(LAST):
            pltpu.make_async_remote_copy(
                src_ref=residual, dst_ref=residuals.at[r],
                send_sem=residual_send.at[0], recv_sem=residual_recv.at[r],
                device_id=(LAST, col), device_id_type=MESH).wait_recv()
        start = [dot_t(residuals[r], dinv[r * BS:(r + 1) * BS, :]) for r in range(ROWS)]
        done = []
        for r in range(ROWS):
            for piece in PIECES:
                if piece[0] == r:
                    straight_copy(piece).wait_recv()
            block = start[r]
            blocks = [factor[r, j] if r < LAST else scaled[j] for j in range(r)]
            if r > 1:
                block -= dot_t(jnp.concatenate(done[:-1], 1), jnp.concatenate(blocks[:-1], 1))
            if r:
                block -= dot_t(done[-1], blocks[-1])
            block = block.astype(BF16)
            done.append(block)
            solved[r] = block
            if r < LAST:
                for to_core in range(2):
                    solved_copy(r, to_core).start()
            else:
                solved_copy(r, 1).start()
                result[mine] = block

    @pl.when(even)
    def _():
        @pl.when(jnp.logical_not(solver))
        def _():
            result_wait(mine)

        for step in FAR_FIRST:
            result_copy(step).start()

    for step in range(1, SOLVERS):
        result_wait(lax.rem(mine + step, SOLVERS))

    @pl.when(jnp.logical_not(even))
    def _():
        result_wait(mine)

    out[...] = result[...].reshape(WIDTH, BS)

    for piece in STRAIGHT:
        @pl.when(owner & (row == piece[0]))
        def _():
            straight_copy(piece).wait_send()

    for via, pieces in VIA.items():
        for piece in pieces:
            @pl.when(owner & (row == piece[0]))
            def _():
                first_leg(piece, via, 1).wait_send()

            @pl.when(helper & (row == via))
            def _():
                second_leg(piece, 0).wait_send()

    for piece in UP + DOWN:
        @pl.when(side & (row == piece[0]))
        def _():
            first_leg(piece, LAST).wait_send()

        @pl.when(side & (row == LAST))
        def _():
            second_leg(piece, 1).wait_send()

    for step in (2, 3, 1):
        part_copy(step).wait_send()

    @pl.when(jnp.logical_not(owner))
    def _():
        part_copy(0).wait_send()

    @pl.when(even)
    def _():
        for step in FAR_FIRST:
            result_copy(step).wait_send()

    @pl.when(owner & (row != LAST))
    def _():
        residual_copy().wait_send()

    @pl.when(solver)
    def _():
        for r in range(ROWS):
            for to_core in range(2):
                if r < LAST or to_core:
                    solved_copy(r, to_core).wait_send()


def on_device(
    rhs, sep_lower, sep_pattern, diag_inverse, child_lower, child_ids, child_count, child_x
):
    dma = pltpu.SemaphoreType.DMA
    found = pl.pallas_call(
        kernel,
        out_shape=pltpu.VMEM((WIDTH, BS), BF16),
        in_specs=[pl.BlockSpec(memory_space=pltpu.HBM)] * 8,
        out_specs=pl.BlockSpec(memory_space=pltpu.VMEM),
        scratch_shapes=[
            pltpu.SMEM((ROWS, ROWS), jnp.int32),
            pltpu.SMEM((1, SLOTS), jnp.int32),
            pltpu.SMEM((1, 1), jnp.int32),
            pltpu.VMEM((BLOCKS + 1, BS, WIDTH), BF16),
            pltpu.VMEM((CHUNKS, BS, SLOTS * BS // CHUNKS), BF16),
            pltpu.VMEM((BS, ROWS * BS), BF16),
            pltpu.VMEM((ROWS * BS, BS), BF16),
            pltpu.VMEM((BS, WIDTH), F32),
            pltpu.VMEM((LAST, BS, BS), BF16),
            pltpu.VMEM((LAST, LAST - 1, BS, BS), BF16),
            pltpu.VMEM((RELAY_BLOCKS, BS, BS), BF16),
            pltpu.VMEM((SOLVERS, PART, BS), BF16),
            pltpu.VMEM((COLS, PART, BS), BF16),
            pltpu.VMEM((SOLVERS, PART, BS), F32),
            pltpu.VMEM((PART, BS), BF16),
            pltpu.VMEM((ROWS, PART, BS), BF16),
            pltpu.VMEM((ROWS, PART, BS), BF16),
            pltpu.VMEM((SOLVERS, PART, BS), BF16),
            dma((7 + CHUNKS,)),
            dma((len(PIECES),)),
            dma((len(PIECES),)),
            dma((len(PIECES),)),
            dma((len(PIECES),)),
            dma((SOLVERS,)),
            dma((COLS,)),
            dma((1,)),
            dma((ROWS,)),
            dma((ROWS, 2)),
            dma((CHIPS,)),
            dma((SOLVERS,)),
        ],
        compiler_params=pltpu.CompilerParams(
            collective_id=0, has_side_effects=True, vmem_limit_bytes=60 * 2**20
        ),
    )(
        sep_pattern, child_ids, child_count, rhs, sep_lower, diag_inverse, child_lower,
        child_x.reshape(BLOCKS, BS, WIDTH),
    )
    return found.T


def solution(mesh):
    in_specs = (
        P("row", None),
        P("row", None),
        P(),
        P(),
        P("row", "col"),
        P("row", "col"),
        P("row", "col"),
        P("col", None),
    )
    return jax.shard_map(
        on_device, mesh=mesh, in_specs=in_specs, out_specs=P("row", None), check_vma=False
    )
```

```python
import jax
import jax.numpy as jnp
from jax import lax
from jax.experimental import pallas as pl
from jax.experimental.pallas import tpu as pltpu
from jax.sharding import PartitionSpec as P

MESH = pl.DeviceIdType.MESH
BF16 = jnp.bfloat16
F32 = jnp.float32

ROWS = 16
COLS = 16
CHIPS = COLS // 2
SOLVERS = CHIPS // 2
BS = 128
WIDTH = 256
PART = WIDTH // SOLVERS
LAST = ROWS - 1
EARLY = 2
SLOTS = 64
BLOCKS = 32
CHUNKS = 4
FAR_FIRST = (4, 3, 5, 2, 6, 1, 7)

VIA = {12: [(8, 0, 4, 0), (8, 4, 8, 4)], 14: [(10, 0, 5, 0), (10, 5, 10, 5)]}
UP = [(6, 0, 2, 0), (6, 2, 4, 2), (6, 4, 6, 4), (12, 0, 3, 6), (12, 3, 6, 9)]
DOWN = [(7, 0, 2, 12), (7, 2, 4, 14), (7, 4, 7, 16), (12, 6, 9, 19), (12, 9, 12, 22)]
SIDE = sorted({piece[0] for piece in UP + DOWN})
ROUTED = {piece[0] for pieces in VIA.values() for piece in pieces} | set(SIDE)
STRAIGHT = [(r, 0, r, 0) for r in range(1, LAST) if r not in ROUTED]
PIECES = STRAIGHT + [piece for pieces in VIA.values() for piece in pieces] + UP + DOWN
RELAY_BLOCKS = 40
GROUPS = (range(0, 4), range(4, 8), range(8, 12), range(12, 16))


def dot_t(a, b):
    return lax.dot_general(a, b, (((1,), (1,)), ((), ())), preferred_element_type=F32)


def any_of(value, options):
    found = value == options[0]
    for option in options[1:]:
        found = found | (value == option)
    return found


def kernel(
    pattern_hbm, ids_hbm, count_hbm, rhs_hbm, sep_hbm, dinv_hbm, lower_hbm, x_hbm, out,
    pattern, ids, count, x_all, lower, sep, dinv, rhs, scaled, factor, relay, own_sum, given, sums,
    parts, base,
    residual, residuals, solved, result,
    load_sem, factor_send, factor_recv, relay_send, relay_recv, give_send, give_recv, part_send, part_recv,
    residual_send, residual_recv, solved_send, result_send, result_recv,
):
    row, col = lax.axis_index("row"), lax.axis_index("col")
    chip, core = col // 2, lax.rem(col, 2)
    mine = chip // 2
    even = lax.rem(chip, 2) == 0
    first = core == 0
    owner = first & even
    reducer = even & (core == 1)
    solver = owner & (row == LAST)
    side = first & jnp.logical_not(even)

    def other_chip(step):
        return lax.rem(chip + step, CHIPS)

    barrier = pltpu.get_barrier_semaphore()

    def greet(r, c):
        pl.semaphore_signal(barrier, inc=1, device_id=(r, c), device_id_type=MESH)

    @pl.when(first)
    def _():
        for step in (2, 3, 1, 0):
            greet(row, 4 * lax.rem(mine + step, SOLVERS) + 1)

        @pl.when(solver)
        def _():
            for r in range(LAST):
                greet(r, col)
            for r in range(ROWS):
                greet(r, 2 * chip + 1)
            for step in (1, CHIPS - 1):
                greet(LAST, 2 * other_chip(step))

        @pl.when(side & (row == LAST))
        def _():
            for r in SIDE:
                greet(r, col)

        for via, pieces in VIA.items():
            @pl.when(owner & (row == via))
            def _():
                for r in sorted({piece[0] for piece in pieces}):
                    greet(r, col)

    @pl.when(core == 1)
    def _():
        greet(row, 2 * chip)

        @pl.when(even)
        def _():
            for step in FAR_FIRST:
                greet(row, 2 * other_chip(step) + 1)
            greet(LAST, 2 * chip)

        @pl.when(jnp.logical_not(even))
        def _():
            for step in (3, 5, 1, 7):
                greet(row, 2 * other_chip(step) + 1)

    def load(src, dst, sem):
        copy = pltpu.make_async_copy(src, dst, load_sem.at[sem])
        copy.start()
        return copy

    load_sep = load(sep_hbm, sep, 0)
    load_dinv = load(dinv_hbm, dinv, 1)
    load_x = load(x_hbm, x_all.at[pl.ds(0, BLOCKS)], 2)
    load_small = [
        load(src, dst, 4 + i)
        for i, (src, dst) in enumerate([(pattern_hbm, pattern), (ids_hbm, ids), (count_hbm, count)])
    ]
    span = SLOTS * BS // CHUNKS
    load_lower = [
        load(lower_hbm.at[:, pl.ds(i * span, span)], lower.at[i], 7 + i) for i in range(CHUNKS)
    ]
    load_rhs = load(rhs_hbm, rhs, 3)
    x_all[BLOCKS] = jnp.zeros((BS, WIDTH), BF16)
    for copy in load_small:
        copy.wait()

    load_sep.wait()
    load_dinv.wait()

    @pl.when(first)
    def _():
        own = dinv[pl.ds(pl.multiple_of(row * BS, BS), BS), :]
        for j in range(LAST):
            term = jnp.dot(own, sep[:, j * BS:(j + 1) * BS], preferred_element_type=F32)
            scaled[j] = (term * pattern[row, j].astype(F32)).astype(BF16)

    def straight_copy(piece):
        r, lo, hi, _ = piece
        i = PIECES.index(piece)
        return pltpu.make_async_remote_copy(
            src_ref=scaled.at[pl.ds(lo, hi - lo)], dst_ref=factor.at[r, pl.ds(lo, hi - lo)],
            send_sem=factor_send.at[i], recv_sem=factor_recv.at[i],
            device_id=(LAST, col), device_id_type=MESH)

    def first_leg(piece, via):
        _, lo, hi, at = piece
        i = PIECES.index(piece)
        return pltpu.make_async_remote_copy(
            src_ref=scaled.at[pl.ds(lo, hi - lo)], dst_ref=relay.at[pl.ds(at, hi - lo)],
            send_sem=factor_send.at[i], recv_sem=relay_recv.at[i],
            device_id=(via, col), device_id_type=MESH)

    def second_leg(piece, to):
        r, lo, hi, at = piece
        i = PIECES.index(piece)
        return pltpu.make_async_remote_copy(
            src_ref=relay.at[pl.ds(at, hi - lo)], dst_ref=factor.at[r, pl.ds(lo, hi - lo)],
            send_sem=relay_send.at[i], recv_sem=factor_recv.at[i],
            device_id=(LAST, 2 * other_chip(to)), device_id_type=MESH)

    def pass_on(piece, to):
        first_leg(piece, LAST).wait_recv()
        second_leg(piece, to).start()

    load_x.wait()
    live = count[0, 0]
    pairs = SLOTS // 2 // CHUNKS

    def child_sum(total, chunks):
        for i in chunks:
            load_lower[i].wait()
            for p in range(pairs):
                j = 2 * (i * pairs + p)
                picked = [x_all[jnp.where(s < live, ids[0, s], BLOCKS)] for s in (j, j + 1)]
                total += jnp.dot(
                    lower[i, :, 2 * p * BS:2 * (p + 1) * BS],
                    jnp.concatenate(picked, 0),
                    preferred_element_type=F32,
                )
        return total

    total = child_sum(jnp.zeros((BS, WIDTH), F32), range(EARLY))

    @pl.when(first)
    def _():
        greeted = 1 + jnp.where(even, jnp.where(row == LAST, ROWS, 1), 0)
        for via, pieces in VIA.items():
            greeted += jnp.where(even & any_of(row, sorted({piece[0] for piece in pieces})), 1, 0)
        greeted += jnp.where(side & any_of(row, SIDE), 1, 0)
        greeted += jnp.where(side & (row == LAST), 2, 0)
        pl.semaphore_wait(barrier, greeted)
        for piece in STRAIGHT:
            @pl.when(owner & (row == piece[0]))
            def _():
                straight_copy(piece).start()

        for via, pieces in VIA.items():
            for piece in pieces:
                @pl.when(owner & (row == piece[0]))
                def _():
                    first_leg(piece, via).start()

        for piece in UP + DOWN:
            @pl.when(side & (row == piece[0]))
            def _():
                first_leg(piece, LAST).start()

    total = child_sum(total, range(EARLY, CHUNKS))
    load_rhs.wait()

    def give_copy():
        return pltpu.make_async_remote_copy(
            src_ref=own_sum, dst_ref=given, send_sem=give_send.at[0], recv_sem=give_recv.at[0],
            device_id=(row, 2 * chip + 1), device_id_type=MESH)

    @pl.when(first)
    def _():
        own_sum[...] = total.T.reshape(SOLVERS, PART, BS)
        give_copy().start()

    @pl.when(core == 1)
    def _():
        own_sum[...] = total.T.reshape(SOLVERS, PART, BS)
        base[...] = rhs[...].T.reshape(SOLVERS, PART, BS)
        pl.semaphore_wait(barrier, jnp.where(even, 2 * CHIPS, SOLVERS))
        give_copy().wait_recv()
        both = own_sum[...] + given[...]
        sums[...] = both.astype(BF16)
        base[...] -= both

    def part_copy(step):
        to = lax.rem(mine + step, SOLVERS)
        return pltpu.make_async_remote_copy(
            src_ref=sums.at[to], dst_ref=parts.at[chip],
            send_sem=part_send.at[step], recv_sem=part_recv.at[chip],
            device_id=(row, 4 * to + 1), device_id_type=MESH)

    @pl.when(core == 1)
    def _():
        for step in (2, 3, 1):
            part_copy(step).start()

        @pl.when(jnp.logical_not(even))
        def _():
            part_copy(0).start()

    def residual_copy():
        return pltpu.make_async_remote_copy(
            src_ref=residual, dst_ref=residuals.at[row],
            send_sem=residual_send.at[0], recv_sem=residual_recv.at[row],
            device_id=(LAST, 2 * chip), device_id_type=MESH)

    def result_copy(step, to_core):
        return pltpu.make_async_remote_copy(
            src_ref=result.at[mine], dst_ref=result.at[mine],
            send_sem=result_send.at[step, to_core], recv_sem=result_recv.at[mine],
            device_id=(row, 2 * other_chip(step) + to_core), device_id_type=MESH)

    def solved_copy(r):
        return pltpu.make_async_remote_copy(
            src_ref=solved.at[r], dst_ref=result.at[mine],
            send_sem=solved_send.at[r], recv_sem=result_recv.at[mine],
            device_id=(r, 2 * chip + 1), device_id_type=MESH)

    def result_wait(at):
        pltpu.make_async_remote_copy(
            src_ref=solved.at[0], dst_ref=result.at[at],
            send_sem=result_send.at[0, 0], recv_sem=result_recv.at[at],
            device_id=(row, col), device_id_type=MESH).wait_recv()

    @pl.when(side & (row == LAST))
    def _():
        for i in range(max(len(UP), len(DOWN))):
            for piece in UP[i:i + 1]:
                pass_on(piece, CHIPS - 1)
            for piece in DOWN[i:i + 1]:
                pass_on(piece, 1)

    for via, pieces in VIA.items():
        @pl.when(owner & (row == via))
        def _():
            for piece in pieces:
                pass_on(piece, 0)

    @pl.when(reducer)
    def _():
        for k in range(1, CHIPS):
            src = other_chip(k)
            pltpu.make_async_remote_copy(
                src_ref=sums.at[0], dst_ref=parts.at[src],
                send_sem=part_send.at[0], recv_sem=part_recv.at[src],
                device_id=(row, col), device_id_type=MESH).wait_recv()
        value = base[mine]
        for k in range(1, CHIPS):
            value -= parts[other_chip(k)].astype(F32)
        residual[...] = value.astype(BF16)
        residual_copy().start()

    @pl.when(solver)
    def _():
        done = []
        for group in GROUPS:
            for r in group:
                pltpu.make_async_remote_copy(
                    src_ref=residual, dst_ref=residuals.at[r],
                    send_sem=residual_send.at[0], recv_sem=residual_recv.at[r],
                    device_id=(LAST, col), device_id_type=MESH).wait_recv()
                for piece in PIECES:
                    if piece[0] == r:
                        straight_copy(piece).wait_recv()
            blocks = {r: [factor[r, j] if r < LAST else scaled[j] for j in range(r)] for r in group}
            start = {r: dot_t(residuals[r], dinv[r * BS:(r + 1) * BS, :]) for r in group}
            top = group[0]
            if top:
                known = jnp.concatenate(done, 1)
                for r in group:
                    start[r] -= dot_t(known, jnp.concatenate(blocks[r][:top], 1))
            for r in group:
                block = start[r]
                if r - top > 1:
                    block -= dot_t(
                        jnp.concatenate(done[top:r - 1], 1), jnp.concatenate(blocks[r][top:r - 1], 1))
                if r > top:
                    block -= dot_t(done[r - 1], blocks[r][r - 1])
                block = block.astype(BF16)
                done.append(block)
                solved[r] = block
                solved_copy(r).start()

    @pl.when(reducer)
    def _():
        result_wait(mine)
        for step in FAR_FIRST:
            for to_core in (1, 0):
                result_copy(step, to_core).start()
        result_copy(0, 0).start()

    for step in range(1, SOLVERS):
        result_wait(lax.rem(mine + step, SOLVERS))

    @pl.when(jnp.logical_not(reducer))
    def _():
        result_wait(mine)

    out[...] = result[...].reshape(WIDTH, BS)

    for piece in STRAIGHT:
        @pl.when(owner & (row == piece[0]))
        def _():
            straight_copy(piece).wait_send()

    for via, pieces in VIA.items():
        for piece in pieces:
            @pl.when(owner & (row == piece[0]))
            def _():
                first_leg(piece, via).wait_send()

            @pl.when(owner & (row == via))
            def _():
                second_leg(piece, 0).wait_send()

    for piece in UP + DOWN:
        @pl.when(side & (row == piece[0]))
        def _():
            first_leg(piece, LAST).wait_send()

        @pl.when(side & (row == LAST))
        def _():
            second_leg(piece, 1).wait_send()

    @pl.when(first)
    def _():
        give_copy().wait_send()

    @pl.when(core == 1)
    def _():
        for step in (2, 3, 1):
            part_copy(step).wait_send()

        @pl.when(jnp.logical_not(even))
        def _():
            part_copy(0).wait_send()

    @pl.when(reducer)
    def _():
        residual_copy().wait_send()
        for step in FAR_FIRST:
            for to_core in (1, 0):
                result_copy(step, to_core).wait_send()
        result_copy(0, 0).wait_send()

    @pl.when(solver)
    def _():
        for r in range(ROWS):
            solved_copy(r).wait_send()


def on_device(
    rhs, sep_lower, sep_pattern, diag_inverse, child_lower, child_ids, child_count, child_x
):
    dma = pltpu.SemaphoreType.DMA
    found = pl.pallas_call(
        kernel,
        out_shape=pltpu.VMEM((WIDTH, BS), BF16),
        in_specs=[pl.BlockSpec(memory_space=pltpu.HBM)] * 8,
        out_specs=pl.BlockSpec(memory_space=pltpu.VMEM),
        scratch_shapes=[
            pltpu.SMEM((ROWS, ROWS), jnp.int32),
            pltpu.SMEM((1, SLOTS), jnp.int32),
            pltpu.SMEM((1, 1), jnp.int32),
            pltpu.VMEM((BLOCKS + 1, BS, WIDTH), BF16),
            pltpu.VMEM((CHUNKS, BS, SLOTS * BS // CHUNKS), BF16),
            pltpu.VMEM((BS, ROWS * BS), BF16),
            pltpu.VMEM((ROWS * BS, BS), BF16),
            pltpu.VMEM((BS, WIDTH), F32),
            pltpu.VMEM((LAST, BS, BS), BF16),
            pltpu.VMEM((LAST, LAST - 1, BS, BS), BF16),
            pltpu.VMEM((RELAY_BLOCKS, BS, BS), BF16),
            pltpu.VMEM((SOLVERS, PART, BS), F32),
            pltpu.VMEM((SOLVERS, PART, BS), F32),
            pltpu.VMEM((SOLVERS, PART, BS), BF16),
            pltpu.VMEM((CHIPS, PART, BS), BF16),
            pltpu.VMEM((SOLVERS, PART, BS), F32),
            pltpu.VMEM((PART, BS), BF16),
            pltpu.VMEM((ROWS, PART, BS), BF16),
            pltpu.VMEM((ROWS, PART, BS), BF16),
            pltpu.VMEM((SOLVERS, PART, BS), BF16),
            dma((7 + CHUNKS,)),
            dma((len(PIECES),)),
            dma((len(PIECES),)),
            dma((len(PIECES),)),
            dma((len(PIECES),)),
            dma((1,)),
            dma((1,)),
            dma((SOLVERS,)),
            dma((CHIPS,)),
            dma((1,)),
            dma((ROWS,)),
            dma((ROWS,)),
            dma((CHIPS, 2)),
            dma((SOLVERS,)),
        ],
        compiler_params=pltpu.CompilerParams(
            collective_id=0, has_side_effects=True, vmem_limit_bytes=60 * 2**20
        ),
    )(
        sep_pattern, child_ids, child_count, rhs, sep_lower, diag_inverse, child_lower,
        child_x.reshape(BLOCKS, BS, WIDTH),
    )
    return found.T


def solution(mesh):
    in_specs = (
        P("row", None),
        P("row", None),
        P(),
        P(),
        P("row", "col"),
        P("row", "col"),
        P("row", "col"),
        P("col", None),
    )
    return jax.shard_map(
        on_device, mesh=mesh, in_specs=in_specs, out_specs=P("row", None), check_vma=False
    )
```

```python
import jax
import jax.numpy as jnp
from jax import lax
from jax.experimental import pallas as pl
from jax.experimental.pallas import tpu as pltpu
from jax.sharding import PartitionSpec as P

MESH = pl.DeviceIdType.MESH
BF16 = jnp.bfloat16
F32 = jnp.float32

ROWS = 16
COLS = 16
CHIPS = COLS // 2
SOLVERS = CHIPS // 2
BS = 128
WIDTH = 256
PART = WIDTH // SOLVERS
LAST = ROWS - 1
EARLY = 2
SLOTS = 64
BLOCKS = 32
CHUNKS = 4
FAR_FIRST = (4, 3, 5, 2, 6, 1, 7)

VIA = {12: [(8, 0, 4, 0), (8, 4, 8, 4)], 14: [(6, 0, 3, 0), (6, 3, 6, 3), (10, 5, 10, 6)]}
UP = [(7, 0, 2, 0), (7, 2, 3, 2), (10, 0, 3, 3), (10, 3, 5, 6), (12, 0, 4, 8)]
DOWN = [(7, 3, 5, 12), (7, 5, 7, 14), (12, 4, 8, 16), (12, 8, 12, 20)]
SIDE = sorted({piece[0] for piece in UP + DOWN})
ROUTED = {piece[0] for pieces in VIA.values() for piece in pieces} | set(SIDE)
STRAIGHT = [(r, 0, r, 0) for r in range(1, LAST) if r not in ROUTED]
PIECES = STRAIGHT + [piece for pieces in VIA.values() for piece in pieces] + UP + DOWN
RELAY_BLOCKS = 40
GROUPS = (range(0, 4), range(4, 6), range(6, 8), range(8, 10), range(10, 12), range(12, 16))


def dot_t(a, b):
    return lax.dot_general(a, b, (((1,), (1,)), ((), ())), preferred_element_type=F32)


def any_of(value, options):
    found = value == options[0]
    for option in options[1:]:
        found = found | (value == option)
    return found


def kernel(
    pattern_hbm, ids_hbm, count_hbm, rhs_hbm, sep_hbm, dinv_hbm, lower_hbm, x_hbm, out,
    pattern, ids, count, x_all, lower, sep, dinv, rhs, scaled, factor, relay, own_sum, given, sums,
    parts, base,
    residual, residuals, solved, result,
    load_sem, factor_send, factor_recv, relay_send, relay_recv, give_send, give_recv, part_send, part_recv,
    residual_send, residual_recv, solved_send, result_send, result_recv,
):
    row, col = lax.axis_index("row"), lax.axis_index("col")
    chip, core = col // 2, lax.rem(col, 2)
    mine = chip // 2
    even = lax.rem(chip, 2) == 0
    first = core == 0
    owner = first & even
    reducer = even & (core == 1)
    solver = owner & (row == LAST)
    side = first & jnp.logical_not(even)

    def other_chip(step):
        return lax.rem(chip + step, CHIPS)

    barrier = pltpu.get_barrier_semaphore()

    def greet(r, c):
        pl.semaphore_signal(barrier, inc=1, device_id=(r, c), device_id_type=MESH)

    @pl.when(first)
    def _():
        for step in (2, 3, 1, 0):
            greet(row, 4 * lax.rem(mine + step, SOLVERS) + 1)

        @pl.when(solver)
        def _():
            for r in range(LAST):
                greet(r, col)
            for r in range(ROWS):
                greet(r, 2 * chip + 1)
            for step in (1, CHIPS - 1):
                greet(LAST, 2 * other_chip(step))

        @pl.when(side & (row == LAST))
        def _():
            for r in SIDE:
                greet(r, col)

        for via, pieces in VIA.items():
            @pl.when(owner & (row == via))
            def _():
                for r in sorted({piece[0] for piece in pieces}):
                    greet(r, col)

    @pl.when(core == 1)
    def _():
        greet(row, 2 * chip)

        @pl.when(even)
        def _():
            for step in FAR_FIRST:
                greet(row, 2 * other_chip(step) + 1)
            greet(LAST, 2 * chip)

        @pl.when(jnp.logical_not(even))
        def _():
            for step in (3, 5, 1, 7):
                greet(row, 2 * other_chip(step) + 1)

    def load(src, dst, sem):
        copy = pltpu.make_async_copy(src, dst, load_sem.at[sem])
        copy.start()
        return copy

    load_sep = load(sep_hbm, sep, 0)
    load_dinv = load(dinv_hbm, dinv, 1)
    load_x = load(x_hbm, x_all.at[pl.ds(0, BLOCKS)], 2)
    load_small = [
        load(src, dst, 4 + i)
        for i, (src, dst) in enumerate([(pattern_hbm, pattern), (ids_hbm, ids), (count_hbm, count)])
    ]
    span = SLOTS * BS // CHUNKS
    load_lower = [
        load(lower_hbm.at[:, pl.ds(i * span, span)], lower.at[i], 7 + i) for i in range(CHUNKS)
    ]
    load_rhs = load(rhs_hbm, rhs, 3)
    x_all[BLOCKS] = jnp.zeros((BS, WIDTH), BF16)
    for copy in load_small:
        copy.wait()

    load_sep.wait()
    load_dinv.wait()

    @pl.when(first)
    def _():
        own = dinv[pl.ds(pl.multiple_of(row * BS, BS), BS), :]
        for j in range(LAST):
            term = jnp.dot(own, sep[:, j * BS:(j + 1) * BS], preferred_element_type=F32)
            scaled[j] = (term * pattern[row, j].astype(F32)).astype(BF16)

    def straight_copy(piece):
        r, lo, hi, _ = piece
        i = PIECES.index(piece)
        return pltpu.make_async_remote_copy(
            src_ref=scaled.at[pl.ds(lo, hi - lo)], dst_ref=factor.at[r, pl.ds(lo, hi - lo)],
            send_sem=factor_send.at[i], recv_sem=factor_recv.at[i],
            device_id=(LAST, col), device_id_type=MESH)

    def first_leg(piece, via):
        _, lo, hi, at = piece
        i = PIECES.index(piece)
        return pltpu.make_async_remote_copy(
            src_ref=scaled.at[pl.ds(lo, hi - lo)], dst_ref=relay.at[pl.ds(at, hi - lo)],
            send_sem=factor_send.at[i], recv_sem=relay_recv.at[i],
            device_id=(via, col), device_id_type=MESH)

    def second_leg(piece, to):
        r, lo, hi, at = piece
        i = PIECES.index(piece)
        return pltpu.make_async_remote_copy(
            src_ref=relay.at[pl.ds(at, hi - lo)], dst_ref=factor.at[r, pl.ds(lo, hi - lo)],
            send_sem=relay_send.at[i], recv_sem=factor_recv.at[i],
            device_id=(LAST, 2 * other_chip(to)), device_id_type=MESH)

    def pass_on(piece, to):
        first_leg(piece, LAST).wait_recv()
        second_leg(piece, to).start()

    load_x.wait()
    live = count[0, 0]
    pairs = SLOTS // 2 // CHUNKS

    def child_sum(total, chunks):
        for i in chunks:
            load_lower[i].wait()
            for p in range(pairs):
                j = 2 * (i * pairs + p)
                picked = [x_all[jnp.where(s < live, ids[0, s], BLOCKS)] for s in (j, j + 1)]
                total += jnp.dot(
                    lower[i, :, 2 * p * BS:2 * (p + 1) * BS],
                    jnp.concatenate(picked, 0),
                    preferred_element_type=F32,
                )
        return total

    total = child_sum(jnp.zeros((BS, WIDTH), F32), range(EARLY))

    @pl.when(first)
    def _():
        greeted = 1 + jnp.where(even, jnp.where(row == LAST, ROWS, 1), 0)
        for via, pieces in VIA.items():
            greeted += jnp.where(even & any_of(row, sorted({piece[0] for piece in pieces})), 1, 0)
        greeted += jnp.where(side & any_of(row, SIDE), 1, 0)
        greeted += jnp.where(side & (row == LAST), 2, 0)
        pl.semaphore_wait(barrier, greeted)
        for piece in STRAIGHT:
            @pl.when(owner & (row == piece[0]))
            def _():
                straight_copy(piece).start()

        for via, pieces in VIA.items():
            for piece in pieces:
                @pl.when(owner & (row == piece[0]))
                def _():
                    first_leg(piece, via).start()

        for piece in UP + DOWN:
            @pl.when(side & (row == piece[0]))
            def _():
                first_leg(piece, LAST).start()

    total = child_sum(total, range(EARLY, CHUNKS))
    load_rhs.wait()

    def give_copy():
        return pltpu.make_async_remote_copy(
            src_ref=own_sum, dst_ref=given, send_sem=give_send.at[0], recv_sem=give_recv.at[0],
            device_id=(row, 2 * chip + 1), device_id_type=MESH)

    @pl.when(first)
    def _():
        own_sum[...] = total.T.reshape(SOLVERS, PART, BS)
        give_copy().start()

    @pl.when(core == 1)
    def _():
        own_sum[...] = total.T.reshape(SOLVERS, PART, BS)
        base[...] = rhs[...].T.reshape(SOLVERS, PART, BS)
        pl.semaphore_wait(barrier, jnp.where(even, 2 * CHIPS, SOLVERS))
        give_copy().wait_recv()
        both = own_sum[...] + given[...]
        sums[...] = both.astype(BF16)
        base[...] -= both

    def part_copy(step):
        to = lax.rem(mine + step, SOLVERS)
        return pltpu.make_async_remote_copy(
            src_ref=sums.at[to], dst_ref=parts.at[chip],
            send_sem=part_send.at[step], recv_sem=part_recv.at[chip],
            device_id=(row, 4 * to + 1), device_id_type=MESH)

    @pl.when(core == 1)
    def _():
        for step in (2, 3, 1):
            part_copy(step).start()

        @pl.when(jnp.logical_not(even))
        def _():
            part_copy(0).start()

    def residual_copy():
        return pltpu.make_async_remote_copy(
            src_ref=residual, dst_ref=residuals.at[row],
            send_sem=residual_send.at[0], recv_sem=residual_recv.at[row],
            device_id=(LAST, 2 * chip), device_id_type=MESH)

    def result_copy(step, to_core):
        return pltpu.make_async_remote_copy(
            src_ref=result.at[mine], dst_ref=result.at[mine],
            send_sem=result_send.at[step, to_core], recv_sem=result_recv.at[mine],
            device_id=(row, 2 * other_chip(step) + to_core), device_id_type=MESH)

    def solved_copy(r):
        return pltpu.make_async_remote_copy(
            src_ref=solved.at[r], dst_ref=result.at[mine],
            send_sem=solved_send.at[r], recv_sem=result_recv.at[mine],
            device_id=(r, 2 * chip + 1), device_id_type=MESH)

    def result_wait(at):
        pltpu.make_async_remote_copy(
            src_ref=solved.at[0], dst_ref=result.at[at],
            send_sem=result_send.at[0, 0], recv_sem=result_recv.at[at],
            device_id=(row, col), device_id_type=MESH).wait_recv()

    @pl.when(side & (row == LAST))
    def _():
        for i in range(max(len(UP), len(DOWN))):
            for piece in DOWN[i:i + 1]:
                pass_on(piece, 1)
            for piece in UP[i:i + 1]:
                pass_on(piece, CHIPS - 1)

    for via, pieces in VIA.items():
        @pl.when(owner & (row == via))
        def _():
            for piece in pieces:
                pass_on(piece, 0)

    @pl.when(reducer)
    def _():
        for k in range(1, CHIPS):
            src = other_chip(k)
            pltpu.make_async_remote_copy(
                src_ref=sums.at[0], dst_ref=parts.at[src],
                send_sem=part_send.at[0], recv_sem=part_recv.at[src],
                device_id=(row, col), device_id_type=MESH).wait_recv()
        value = base[mine]
        for k in range(1, CHIPS):
            value -= parts[other_chip(k)].astype(F32)
        residual[...] = value.astype(BF16)
        residual_copy().start()

    @pl.when(solver)
    def _():
        done = []
        for group in GROUPS:
            for r in group:
                pltpu.make_async_remote_copy(
                    src_ref=residual, dst_ref=residuals.at[r],
                    send_sem=residual_send.at[0], recv_sem=residual_recv.at[r],
                    device_id=(LAST, col), device_id_type=MESH).wait_recv()
                for piece in PIECES:
                    if piece[0] == r:
                        straight_copy(piece).wait_recv()
            blocks = {r: [factor[r, j] if r < LAST else scaled[j] for j in range(r)] for r in group}
            start = {r: dot_t(residuals[r], dinv[r * BS:(r + 1) * BS, :]) for r in group}
            top = group[0]
            if top:
                known = jnp.concatenate(done, 1)
                for r in group:
                    start[r] -= dot_t(known, jnp.concatenate(blocks[r][:top], 1))
            for r in group:
                block = start[r]
                if r - top > 1:
                    block -= dot_t(
                        jnp.concatenate(done[top:r - 1], 1), jnp.concatenate(blocks[r][top:r - 1], 1))
                if r > top:
                    block -= dot_t(done[r - 1], blocks[r][r - 1])
                block = block.astype(BF16)
                done.append(block)
                solved[r] = block
                solved_copy(r).start()

    @pl.when(reducer)
    def _():
        result_wait(mine)
        for step in FAR_FIRST:
            for to_core in (1, 0):
                result_copy(step, to_core).start()
        result_copy(0, 0).start()

    for step in range(1, SOLVERS):
        result_wait(lax.rem(mine + step, SOLVERS))

    @pl.when(jnp.logical_not(reducer))
    def _():
        result_wait(mine)

    out[...] = result[...].reshape(WIDTH, BS)

    for piece in STRAIGHT:
        @pl.when(owner & (row == piece[0]))
        def _():
            straight_copy(piece).wait_send()

    for via, pieces in VIA.items():
        for piece in pieces:
            @pl.when(owner & (row == piece[0]))
            def _():
                first_leg(piece, via).wait_send()

            @pl.when(owner & (row == via))
            def _():
                second_leg(piece, 0).wait_send()

    for piece in UP + DOWN:
        @pl.when(side & (row == piece[0]))
        def _():
            first_leg(piece, LAST).wait_send()

        @pl.when(side & (row == LAST))
        def _():
            second_leg(piece, 1).wait_send()

    @pl.when(first)
    def _():
        give_copy().wait_send()

    @pl.when(core == 1)
    def _():
        for step in (2, 3, 1):
            part_copy(step).wait_send()

        @pl.when(jnp.logical_not(even))
        def _():
            part_copy(0).wait_send()

    @pl.when(reducer)
    def _():
        residual_copy().wait_send()
        for step in FAR_FIRST:
            for to_core in (1, 0):
                result_copy(step, to_core).wait_send()
        result_copy(0, 0).wait_send()

    @pl.when(solver)
    def _():
        for r in range(ROWS):
            solved_copy(r).wait_send()


def on_device(
    rhs, sep_lower, sep_pattern, diag_inverse, child_lower, child_ids, child_count, child_x
):
    dma = pltpu.SemaphoreType.DMA
    found = pl.pallas_call(
        kernel,
        out_shape=pltpu.VMEM((WIDTH, BS), BF16),
        in_specs=[pl.BlockSpec(memory_space=pltpu.HBM)] * 8,
        out_specs=pl.BlockSpec(memory_space=pltpu.VMEM),
        scratch_shapes=[
            pltpu.SMEM((ROWS, ROWS), jnp.int32),
            pltpu.SMEM((1, SLOTS), jnp.int32),
            pltpu.SMEM((1, 1), jnp.int32),
            pltpu.VMEM((BLOCKS + 1, BS, WIDTH), BF16),
            pltpu.VMEM((CHUNKS, BS, SLOTS * BS // CHUNKS), BF16),
            pltpu.VMEM((BS, ROWS * BS), BF16),
            pltpu.VMEM((ROWS * BS, BS), BF16),
            pltpu.VMEM((BS, WIDTH), F32),
            pltpu.VMEM((LAST, BS, BS), BF16),
            pltpu.VMEM((LAST, LAST - 1, BS, BS), BF16),
            pltpu.VMEM((RELAY_BLOCKS, BS, BS), BF16),
            pltpu.VMEM((SOLVERS, PART, BS), F32),
            pltpu.VMEM((SOLVERS, PART, BS), F32),
            pltpu.VMEM((SOLVERS, PART, BS), BF16),
            pltpu.VMEM((CHIPS, PART, BS), BF16),
            pltpu.VMEM((SOLVERS, PART, BS), F32),
            pltpu.VMEM((PART, BS), BF16),
            pltpu.VMEM((ROWS, PART, BS), BF16),
            pltpu.VMEM((ROWS, PART, BS), BF16),
            pltpu.VMEM((SOLVERS, PART, BS), BF16),
            dma((7 + CHUNKS,)),
            dma((len(PIECES),)),
            dma((len(PIECES),)),
            dma((len(PIECES),)),
            dma((len(PIECES),)),
            dma((1,)),
            dma((1,)),
            dma((SOLVERS,)),
            dma((CHIPS,)),
            dma((1,)),
            dma((ROWS,)),
            dma((ROWS,)),
            dma((CHIPS, 2)),
            dma((SOLVERS,)),
        ],
        compiler_params=pltpu.CompilerParams(
            collective_id=0, has_side_effects=True, vmem_limit_bytes=60 * 2**20
        ),
    )(
        sep_pattern, child_ids, child_count, rhs, sep_lower, diag_inverse, child_lower,
        child_x.reshape(BLOCKS, BS, WIDTH),
    )
    return found.T


def solution(mesh):
    in_specs = (
        P("row", None),
        P("row", None),
        P(),
        P(),
        P("row", "col"),
        P("row", "col"),
        P("row", "col"),
        P("col", None),
    )
    return jax.shard_map(
        on_device, mesh=mesh, in_specs=in_specs, out_specs=P("row", None), check_vma=False
    )
```

```python
import jax
import jax.numpy as jnp
from jax import lax
from jax.experimental import pallas as pl
from jax.experimental.pallas import tpu as pltpu
from jax.sharding import PartitionSpec as P

MESH = pl.DeviceIdType.MESH
BF16 = jnp.bfloat16
F32 = jnp.float32

ROWS = 16
COLS = 16
CHIPS = COLS // 2
SOLVERS = CHIPS // 2
BS = 128
WIDTH = 256
PART = WIDTH // SOLVERS
LAST = ROWS - 1
EARLY = 2
SLOTS = 64
BLOCKS = 32
CHUNKS = 4
FAR_FIRST = (4, 3, 5, 2, 6, 1, 7)

VIA = {12: [(8, 0, 4, 0), (8, 4, 8, 4)], 14: [(6, 0, 3, 0), (6, 3, 6, 3), (10, 5, 7, 6)]}
UP = [(7, 0, 2, 0), (7, 2, 3, 2), (10, 0, 3, 3), (10, 3, 5, 6), (12, 0, 4, 8)]
DOWN = [(7, 3, 5, 12), (7, 5, 7, 14), (12, 4, 8, 16), (12, 8, 12, 20)]
SIDE = sorted({piece[0] for piece in UP + DOWN})
ROUTED = {piece[0] for pieces in VIA.values() for piece in pieces} | set(SIDE)
STRAIGHT = [(r, 0, r, 0) for r in range(1, LAST) if r not in ROUTED]
STRAIGHT += [(10, 7, 10, 0)]
PIECES = STRAIGHT + [piece for pieces in VIA.values() for piece in pieces] + UP + DOWN
RELAY_BLOCKS = 40
GROUPS = (range(0, 4), range(4, 6), range(6, 8), range(8, 10), range(10, 12), range(12, 16))


def dot_t(a, b):
    return lax.dot_general(a, b, (((1,), (1,)), ((), ())), preferred_element_type=F32)


def any_of(value, options):
    found = value == options[0]
    for option in options[1:]:
        found = found | (value == option)
    return found


def kernel(
    pattern_hbm, ids_hbm, count_hbm, rhs_hbm, sep_hbm, dinv_hbm, lower_hbm, x_hbm, out,
    pattern, ids, count, x_all, lower, sep, dinv, rhs, scaled, factor, relay, own_sum, given, sums,
    parts, base,
    residual, residuals, solved, result,
    load_sem, factor_send, factor_recv, relay_send, relay_recv, give_send, give_recv, part_send, part_recv,
    residual_send, residual_recv, solved_send, result_send, result_recv,
):
    row, col = lax.axis_index("row"), lax.axis_index("col")
    chip, core = col // 2, lax.rem(col, 2)
    mine = chip // 2
    even = lax.rem(chip, 2) == 0
    first = core == 0
    owner = first & even
    reducer = even & (core == 1)
    solver = owner & (row == LAST)
    side = first & jnp.logical_not(even)

    def other_chip(step):
        return lax.rem(chip + step, CHIPS)

    barrier = pltpu.get_barrier_semaphore()

    def greet(r, c):
        pl.semaphore_signal(barrier, inc=1, device_id=(r, c), device_id_type=MESH)

    @pl.when(first)
    def _():
        @pl.when(solver)
        def _():
            for r in (5, 6, 9, 1, 4, 2, 7, 8, 10, 13, 3, 11, 14, 12, 0):
                greet(r, col)
            for step in (1, CHIPS - 1):
                greet(LAST, 2 * other_chip(step))
            for r in range(ROWS):
                greet(r, 2 * chip + 1)

        @pl.when(side & (row == LAST))
        def _():
            for r in SIDE:
                greet(r, col)

        for via, pieces in VIA.items():
            @pl.when(owner & (row == via))
            def _():
                for r in sorted({piece[0] for piece in pieces}):
                    greet(r, col)

        for step in (2, 3, 1, 0):
            greet(row, 4 * lax.rem(mine + step, SOLVERS) + 1)

    @pl.when(core == 1)
    def _():
        greet(row, 2 * chip)

        @pl.when(even)
        def _():
            for step in FAR_FIRST:
                greet(row, 2 * other_chip(step) + 1)
            greet(LAST, 2 * chip)

        @pl.when(jnp.logical_not(even))
        def _():
            for step in (3, 5, 1, 7):
                greet(row, 2 * other_chip(step) + 1)

    def load(src, dst, sem):
        copy = pltpu.make_async_copy(src, dst, load_sem.at[sem])
        copy.start()
        return copy

    load_sep = load(sep_hbm, sep, 0)
    load_dinv = load(dinv_hbm, dinv, 1)
    load_x = load(x_hbm, x_all.at[pl.ds(0, BLOCKS)], 2)
    load_small = [
        load(src, dst, 4 + i)
        for i, (src, dst) in enumerate([(pattern_hbm, pattern), (ids_hbm, ids), (count_hbm, count)])
    ]
    span = SLOTS * BS // CHUNKS
    load_lower = [
        load(lower_hbm.at[:, pl.ds(i * span, span)], lower.at[i], 7 + i) for i in range(CHUNKS)
    ]
    load_rhs = load(rhs_hbm, rhs, 3)
    x_all[BLOCKS] = jnp.zeros((BS, WIDTH), BF16)
    for copy in load_small:
        copy.wait()

    load_sep.wait()
    load_dinv.wait()

    @pl.when(first)
    def _():
        own = dinv[pl.ds(pl.multiple_of(row * BS, BS), BS), :]
        for j in range(LAST):
            term = jnp.dot(own, sep[:, j * BS:(j + 1) * BS], preferred_element_type=F32)
            scaled[j] = (term * pattern[row, j].astype(F32)).astype(BF16)

    def straight_copy(piece):
        r, lo, hi, _ = piece
        i = PIECES.index(piece)
        return pltpu.make_async_remote_copy(
            src_ref=scaled.at[pl.ds(lo, hi - lo)], dst_ref=factor.at[r, pl.ds(lo, hi - lo)],
            send_sem=factor_send.at[i], recv_sem=factor_recv.at[i],
            device_id=(LAST, col), device_id_type=MESH)

    def first_leg(piece, via):
        _, lo, hi, at = piece
        i = PIECES.index(piece)
        return pltpu.make_async_remote_copy(
            src_ref=scaled.at[pl.ds(lo, hi - lo)], dst_ref=relay.at[pl.ds(at, hi - lo)],
            send_sem=factor_send.at[i], recv_sem=relay_recv.at[i],
            device_id=(via, col), device_id_type=MESH)

    def second_leg(piece, to):
        r, lo, hi, at = piece
        i = PIECES.index(piece)
        return pltpu.make_async_remote_copy(
            src_ref=relay.at[pl.ds(at, hi - lo)], dst_ref=factor.at[r, pl.ds(lo, hi - lo)],
            send_sem=relay_send.at[i], recv_sem=factor_recv.at[i],
            device_id=(LAST, 2 * other_chip(to)), device_id_type=MESH)

    def pass_on(piece, to):
        first_leg(piece, LAST).wait_recv()
        second_leg(piece, to).start()

    load_x.wait()
    live = count[0, 0]
    pairs = SLOTS // 2 // CHUNKS

    def child_sum(total, chunks):
        for i in chunks:
            load_lower[i].wait()
            for p in range(pairs):
                j = 2 * (i * pairs + p)
                picked = [x_all[jnp.where(s < live, ids[0, s], BLOCKS)] for s in (j, j + 1)]
                total += jnp.dot(
                    lower[i, :, 2 * p * BS:2 * (p + 1) * BS],
                    jnp.concatenate(picked, 0),
                    preferred_element_type=F32,
                )
        return total

    total = child_sum(jnp.zeros((BS, WIDTH), F32), range(EARLY))

    @pl.when(first)
    def _():
        greeted = 1 + jnp.where(even, jnp.where(row == LAST, ROWS, 1), 0)
        for via, pieces in VIA.items():
            greeted += jnp.where(even & any_of(row, sorted({piece[0] for piece in pieces})), 1, 0)
        greeted += jnp.where(side & any_of(row, SIDE), 1, 0)
        greeted += jnp.where(side & (row == LAST), 2, 0)
        pl.semaphore_wait(barrier, greeted)
        for piece in STRAIGHT:
            @pl.when(owner & (row == piece[0]))
            def _():
                straight_copy(piece).start()

        for via, pieces in VIA.items():
            for piece in pieces:
                @pl.when(owner & (row == piece[0]))
                def _():
                    first_leg(piece, via).start()

        for piece in UP + DOWN:
            @pl.when(side & (row == piece[0]))
            def _():
                first_leg(piece, LAST).start()

    total = child_sum(total, range(EARLY, CHUNKS))
    load_rhs.wait()

    def give_copy():
        return pltpu.make_async_remote_copy(
            src_ref=own_sum, dst_ref=given, send_sem=give_send.at[0], recv_sem=give_recv.at[0],
            device_id=(row, 2 * chip + 1), device_id_type=MESH)

    @pl.when(first)
    def _():
        own_sum[...] = total.T.reshape(SOLVERS, PART, BS)
        give_copy().start()

    @pl.when(core == 1)
    def _():
        own_sum[...] = total.T.reshape(SOLVERS, PART, BS)
        base[...] = rhs[...].T.reshape(SOLVERS, PART, BS)
        pl.semaphore_wait(barrier, jnp.where(even, 2 * CHIPS, SOLVERS))
        give_copy().wait_recv()
        both = own_sum[...] + given[...]
        sums[...] = both.astype(BF16)
        base[...] -= both

    def part_copy(step):
        to = lax.rem(mine + step, SOLVERS)
        return pltpu.make_async_remote_copy(
            src_ref=sums.at[to], dst_ref=parts.at[chip],
            send_sem=part_send.at[step], recv_sem=part_recv.at[chip],
            device_id=(row, 4 * to + 1), device_id_type=MESH)

    @pl.when(core == 1)
    def _():
        for step in (2, 3, 1):
            part_copy(step).start()

        @pl.when(jnp.logical_not(even))
        def _():
            part_copy(0).start()

    def residual_copy():
        return pltpu.make_async_remote_copy(
            src_ref=residual, dst_ref=residuals.at[row],
            send_sem=residual_send.at[0], recv_sem=residual_recv.at[row],
            device_id=(LAST, 2 * chip), device_id_type=MESH)

    def result_copy(step, to_core):
        return pltpu.make_async_remote_copy(
            src_ref=result.at[mine], dst_ref=result.at[mine],
            send_sem=result_send.at[step, to_core], recv_sem=result_recv.at[mine],
            device_id=(row, 2 * other_chip(step) + to_core), device_id_type=MESH)

    def solved_copy(r):
        return pltpu.make_async_remote_copy(
            src_ref=solved.at[r], dst_ref=result.at[mine],
            send_sem=solved_send.at[r], recv_sem=result_recv.at[mine],
            device_id=(r, 2 * chip + 1), device_id_type=MESH)

    def result_wait(at):
        pltpu.make_async_remote_copy(
            src_ref=solved.at[0], dst_ref=result.at[at],
            send_sem=result_send.at[0, 0], recv_sem=result_recv.at[at],
            device_id=(row, col), device_id_type=MESH).wait_recv()

    @pl.when(side & (row == LAST))
    def _():
        for i in range(max(len(UP), len(DOWN))):
            for piece in DOWN[i:i + 1]:
                pass_on(piece, 1)
            for piece in UP[i:i + 1]:
                pass_on(piece, CHIPS - 1)

    for via, pieces in VIA.items():
        @pl.when(owner & (row == via))
        def _():
            for piece in pieces:
                pass_on(piece, 0)

    @pl.when(reducer)
    def _():
        for k in range(1, CHIPS):
            src = other_chip(k)
            pltpu.make_async_remote_copy(
                src_ref=sums.at[0], dst_ref=parts.at[src],
                send_sem=part_send.at[0], recv_sem=part_recv.at[src],
                device_id=(row, col), device_id_type=MESH).wait_recv()
        value = base[mine]
        for k in range(1, CHIPS):
            value -= parts[other_chip(k)].astype(F32)
        residual[...] = value.astype(BF16)
        residual_copy().start()

    @pl.when(solver)
    def _():
        done = []
        for group in GROUPS:
            for r in group:
                pltpu.make_async_remote_copy(
                    src_ref=residual, dst_ref=residuals.at[r],
                    send_sem=residual_send.at[0], recv_sem=residual_recv.at[r],
                    device_id=(LAST, col), device_id_type=MESH).wait_recv()
                for piece in PIECES:
                    if piece[0] == r:
                        straight_copy(piece).wait_recv()
            blocks = {r: [factor[r, j] if r < LAST else scaled[j] for j in range(r)] for r in group}
            start = {r: dot_t(residuals[r], dinv[r * BS:(r + 1) * BS, :]) for r in group}
            top = group[0]
            if top:
                known = jnp.concatenate(done, 1)
                for r in group:
                    start[r] -= dot_t(known, jnp.concatenate(blocks[r][:top], 1))
            for r in group:
                block = start[r]
                if r - top > 1:
                    block -= dot_t(
                        jnp.concatenate(done[top:r - 1], 1), jnp.concatenate(blocks[r][top:r - 1], 1))
                if r > top:
                    block -= dot_t(done[r - 1], blocks[r][r - 1])
                block = block.astype(BF16)
                done.append(block)
                solved[r] = block
                solved_copy(r).start()

    @pl.when(reducer)
    def _():
        result_wait(mine)
        for step in FAR_FIRST:
            for to_core in (1, 0):
                result_copy(step, to_core).start()
        result_copy(0, 0).start()

    for step in range(1, SOLVERS):
        result_wait(lax.rem(mine + step, SOLVERS))

    @pl.when(jnp.logical_not(reducer))
    def _():
        result_wait(mine)

    out[...] = result[...].reshape(WIDTH, BS)

    for piece in STRAIGHT:
        @pl.when(owner & (row == piece[0]))
        def _():
            straight_copy(piece).wait_send()

    for via, pieces in VIA.items():
        for piece in pieces:
            @pl.when(owner & (row == piece[0]))
            def _():
                first_leg(piece, via).wait_send()

            @pl.when(owner & (row == via))
            def _():
                second_leg(piece, 0).wait_send()

    for piece in UP + DOWN:
        @pl.when(side & (row == piece[0]))
        def _():
            first_leg(piece, LAST).wait_send()

        @pl.when(side & (row == LAST))
        def _():
            second_leg(piece, 1).wait_send()

    @pl.when(first)
    def _():
        give_copy().wait_send()

    @pl.when(core == 1)
    def _():
        for step in (2, 3, 1):
            part_copy(step).wait_send()

        @pl.when(jnp.logical_not(even))
        def _():
            part_copy(0).wait_send()

    @pl.when(reducer)
    def _():
        residual_copy().wait_send()
        for step in FAR_FIRST:
            for to_core in (1, 0):
                result_copy(step, to_core).wait_send()
        result_copy(0, 0).wait_send()

    @pl.when(solver)
    def _():
        for r in range(ROWS):
            solved_copy(r).wait_send()


def on_device(
    rhs, sep_lower, sep_pattern, diag_inverse, child_lower, child_ids, child_count, child_x
):
    dma = pltpu.SemaphoreType.DMA
    found = pl.pallas_call(
        kernel,
        out_shape=pltpu.VMEM((WIDTH, BS), BF16),
        in_specs=[pl.BlockSpec(memory_space=pltpu.HBM)] * 8,
        out_specs=pl.BlockSpec(memory_space=pltpu.VMEM),
        scratch_shapes=[
            pltpu.SMEM((ROWS, ROWS), jnp.int32),
            pltpu.SMEM((1, SLOTS), jnp.int32),
            pltpu.SMEM((1, 1), jnp.int32),
            pltpu.VMEM((BLOCKS + 1, BS, WIDTH), BF16),
            pltpu.VMEM((CHUNKS, BS, SLOTS * BS // CHUNKS), BF16),
            pltpu.VMEM((BS, ROWS * BS), BF16),
            pltpu.VMEM((ROWS * BS, BS), BF16),
            pltpu.VMEM((BS, WIDTH), F32),
            pltpu.VMEM((LAST, BS, BS), BF16),
            pltpu.VMEM((LAST, LAST - 1, BS, BS), BF16),
            pltpu.VMEM((RELAY_BLOCKS, BS, BS), BF16),
            pltpu.VMEM((SOLVERS, PART, BS), F32),
            pltpu.VMEM((SOLVERS, PART, BS), F32),
            pltpu.VMEM((SOLVERS, PART, BS), BF16),
            pltpu.VMEM((CHIPS, PART, BS), BF16),
            pltpu.VMEM((SOLVERS, PART, BS), F32),
            pltpu.VMEM((PART, BS), BF16),
            pltpu.VMEM((ROWS, PART, BS), BF16),
            pltpu.VMEM((ROWS, PART, BS), BF16),
            pltpu.VMEM((SOLVERS, PART, BS), BF16),
            dma((7 + CHUNKS,)),
            dma((len(PIECES),)),
            dma((len(PIECES),)),
            dma((len(PIECES),)),
            dma((len(PIECES),)),
            dma((1,)),
            dma((1,)),
            dma((SOLVERS,)),
            dma((CHIPS,)),
            dma((1,)),
            dma((ROWS,)),
            dma((ROWS,)),
            dma((CHIPS, 2)),
            dma((SOLVERS,)),
        ],
        compiler_params=pltpu.CompilerParams(
            collective_id=0, has_side_effects=True, vmem_limit_bytes=60 * 2**20
        ),
    )(
        sep_pattern, child_ids, child_count, rhs, sep_lower, diag_inverse, child_lower,
        child_x.reshape(BLOCKS, BS, WIDTH),
    )
    return found.T


def solution(mesh):
    in_specs = (
        P("row", None),
        P("row", None),
        P(),
        P(),
        P("row", "col"),
        P("row", "col"),
        P("row", "col"),
        P("col", None),
    )
    return jax.shard_map(
        on_device, mesh=mesh, in_specs=in_specs, out_specs=P("row", None), check_vma=False
    )
```

```python
import jax
import jax.numpy as jnp
from jax import lax
from jax.experimental import pallas as pl
from jax.experimental.pallas import tpu as pltpu
from jax.sharding import PartitionSpec as P

MESH = pl.DeviceIdType.MESH
BF16 = jnp.bfloat16
F32 = jnp.float32

ROWS = 16
COLS = 16
CHIPS = COLS // 2
SOLVERS = CHIPS // 2
BS = 128
WIDTH = 256
PART = WIDTH // SOLVERS
LAST = ROWS - 1
EARLY = 2
SLOTS = 64
BLOCKS = 32
CHUNKS = 4
FAR_FIRST = (4, 3, 5, 2, 6, 1, 7)

VIA = {12: [(8, 0, 4, 0), (8, 4, 8, 4)], 14: [(6, 0, 3, 0), (6, 3, 6, 3), (10, 5, 7, 6)]}
UP = [(7, 0, 2, 0), (7, 2, 3, 2), (10, 0, 3, 3), (10, 3, 5, 6), (12, 0, 4, 8)]
DOWN = [(7, 3, 5, 12), (7, 5, 7, 14), (12, 4, 8, 16), (12, 8, 12, 20)]
SIDE = sorted({piece[0] for piece in UP + DOWN})
ROUTED = {piece[0] for pieces in VIA.values() for piece in pieces} | set(SIDE)
STRAIGHT = [(r, 0, r, 0) for r in range(1, LAST) if r not in ROUTED]
STRAIGHT += [(10, 7, 10, 0)]
PIECES = STRAIGHT + [piece for pieces in VIA.values() for piece in pieces] + UP + DOWN
RELAY_BLOCKS = 40
GROUPS = (range(0, 4), range(4, 6), range(6, 8), range(8, 10), range(10, 12), range(12, 16))


def dot_t(a, b):
    return lax.dot_general(a, b, (((1,), (1,)), ((), ())), preferred_element_type=F32)


def any_of(value, options):
    found = value == options[0]
    for option in options[1:]:
        found = found | (value == option)
    return found


def kernel(
    pattern_hbm, ids_hbm, count_hbm, rhs_hbm, sep_hbm, dinv_hbm, lower_hbm, x_hbm, out,
    pattern, ids, count, x_all, lower, sep, dinv, rhs, scaled, factor, relay, own_sum, given, sums,
    parts, base,
    residual, residuals, solved, result,
    load_sem, factor_send, factor_recv, relay_send, relay_recv, give_send, give_recv, part_send, part_recv,
    residual_send, residual_recv, solved_send, result_send, result_recv,
):
    row, col = lax.axis_index("row"), lax.axis_index("col")
    chip, core = col // 2, lax.rem(col, 2)
    mine = chip // 2
    even = lax.rem(chip, 2) == 0
    first = core == 0
    owner = first & even
    reducer = even & (core == 1)
    solver = owner & (row == LAST)
    side = first & jnp.logical_not(even)

    def other_chip(step):
        return lax.rem(chip + step, CHIPS)

    barrier = pltpu.get_barrier_semaphore()

    def greet(r, c):
        pl.semaphore_signal(barrier, inc=1, device_id=(r, c), device_id_type=MESH)

    @pl.when(first)
    def _():
        @pl.when(solver)
        def _():
            for r in (5, 6, 9, 1, 4, 2, 7, 8, 10, 13, 3, 11, 14, 12, 0):
                greet(r, col)
            for step in (1, CHIPS - 1):
                greet(LAST, 2 * other_chip(step))
            for r in range(ROWS):
                greet(r, 2 * chip + 1)

        @pl.when(side & (row == LAST))
        def _():
            for r in SIDE:
                greet(r, col)

        for via, pieces in VIA.items():
            @pl.when(owner & (row == via))
            def _():
                for r in sorted({piece[0] for piece in pieces}):
                    greet(r, col)

        for step in (2, 3, 1, 0):
            greet(row, 4 * lax.rem(mine + step, SOLVERS) + 1)

    @pl.when(core == 1)
    def _():
        greet(row, 2 * chip)

        @pl.when(even)
        def _():
            for step in FAR_FIRST:
                greet(row, 2 * other_chip(step) + 1)
            greet(LAST, 2 * chip)

        @pl.when(jnp.logical_not(even))
        def _():
            for step in (3, 5, 1, 7):
                greet(row, 2 * other_chip(step) + 1)

    def load(src, dst, sem):
        copy = pltpu.make_async_copy(src, dst, load_sem.at[sem])
        copy.start()
        return copy

    load_sep = load(sep_hbm, sep, 0)
    load_dinv = load(dinv_hbm, dinv, 1)
    load_x = load(x_hbm, x_all.at[pl.ds(0, BLOCKS)], 2)
    load_small = [
        load(src, dst, 4 + i)
        for i, (src, dst) in enumerate([(pattern_hbm, pattern), (ids_hbm, ids), (count_hbm, count)])
    ]
    span = SLOTS * BS // CHUNKS
    load_lower = [
        load(lower_hbm.at[:, pl.ds(i * span, span)], lower.at[i], 7 + i) for i in range(CHUNKS)
    ]
    load_rhs = load(rhs_hbm, rhs, 3)
    x_all[BLOCKS] = jnp.zeros((BS, WIDTH), BF16)
    for copy in load_small:
        copy.wait()

    load_sep.wait()
    load_dinv.wait()

    @pl.when(first)
    def _():
        own = dinv[pl.ds(pl.multiple_of(row * BS, BS), BS), :]
        for j in range(LAST):
            term = jnp.dot(own, sep[:, j * BS:(j + 1) * BS], preferred_element_type=F32)
            scaled[j] = (term * pattern[row, j].astype(F32)).astype(BF16)

    def straight_copy(piece):
        r, lo, hi, _ = piece
        i = PIECES.index(piece)
        return pltpu.make_async_remote_copy(
            src_ref=scaled.at[pl.ds(lo, hi - lo)], dst_ref=factor.at[r, pl.ds(lo, hi - lo)],
            send_sem=factor_send.at[i], recv_sem=factor_recv.at[i],
            device_id=(LAST, col), device_id_type=MESH)

    def first_leg(piece, via):
        _, lo, hi, at = piece
        i = PIECES.index(piece)
        return pltpu.make_async_remote_copy(
            src_ref=scaled.at[pl.ds(lo, hi - lo)], dst_ref=relay.at[pl.ds(at, hi - lo)],
            send_sem=factor_send.at[i], recv_sem=relay_recv.at[i],
            device_id=(via, col), device_id_type=MESH)

    def second_leg(piece, to):
        r, lo, hi, at = piece
        i = PIECES.index(piece)
        return pltpu.make_async_remote_copy(
            src_ref=relay.at[pl.ds(at, hi - lo)], dst_ref=factor.at[r, pl.ds(lo, hi - lo)],
            send_sem=relay_send.at[i], recv_sem=factor_recv.at[i],
            device_id=(LAST, 2 * other_chip(to)), device_id_type=MESH)

    def pass_on(piece, to):
        first_leg(piece, LAST).wait_recv()
        second_leg(piece, to).start()

    load_x.wait()
    live = count[0, 0]
    pairs = SLOTS // 2 // CHUNKS

    def child_sum(total, chunks):
        for i in chunks:
            load_lower[i].wait()
            for p in range(pairs):
                j = 2 * (i * pairs + p)
                picked = [x_all[jnp.where(s < live, ids[0, s], BLOCKS)] for s in (j, j + 1)]
                total += jnp.dot(
                    lower[i, :, 2 * p * BS:2 * (p + 1) * BS],
                    jnp.concatenate(picked, 0),
                    preferred_element_type=F32,
                )
        return total

    total = child_sum(jnp.zeros((BS, WIDTH), F32), range(EARLY))

    @pl.when(first)
    def _():
        greeted = 1 + jnp.where(even, jnp.where(row == LAST, ROWS, 1), 0)
        for via, pieces in VIA.items():
            greeted += jnp.where(even & any_of(row, sorted({piece[0] for piece in pieces})), 1, 0)
        greeted += jnp.where(side & any_of(row, SIDE), 1, 0)
        greeted += jnp.where(side & (row == LAST), 2, 0)
        pl.semaphore_wait(barrier, greeted)
        for piece in STRAIGHT:
            @pl.when(owner & (row == piece[0]))
            def _():
                straight_copy(piece).start()

        for via, pieces in VIA.items():
            for piece in pieces:
                @pl.when(owner & (row == piece[0]))
                def _():
                    first_leg(piece, via).start()

        for piece in UP + DOWN:
            @pl.when(side & (row == piece[0]))
            def _():
                first_leg(piece, LAST).start()

    total = child_sum(total, range(EARLY, CHUNKS))
    load_rhs.wait()

    def give_copy():
        return pltpu.make_async_remote_copy(
            src_ref=sums, dst_ref=given, send_sem=give_send.at[0], recv_sem=give_recv.at[0],
            device_id=(row, 2 * chip + 1), device_id_type=MESH)

    @pl.when(first)
    def _():
        sums[...] = total.T.reshape(SOLVERS, PART, BS).astype(BF16)
        give_copy().start()

    @pl.when(core == 1)
    def _():
        own_sum[...] = total.T.reshape(SOLVERS, PART, BS)
        base[...] = rhs[...].T.reshape(SOLVERS, PART, BS)
        pl.semaphore_wait(barrier, jnp.where(even, 2 * CHIPS, SOLVERS))
        give_copy().wait_recv()
        both = own_sum[...] + given[...].astype(F32)
        sums[...] = both.astype(BF16)
        base[...] -= both

    def part_copy(step):
        to = lax.rem(mine + step, SOLVERS)
        return pltpu.make_async_remote_copy(
            src_ref=sums.at[to], dst_ref=parts.at[chip],
            send_sem=part_send.at[step], recv_sem=part_recv.at[chip],
            device_id=(row, 4 * to + 1), device_id_type=MESH)

    @pl.when(core == 1)
    def _():
        for step in (2, 3, 1):
            part_copy(step).start()

        @pl.when(jnp.logical_not(even))
        def _():
            part_copy(0).start()

    def residual_copy():
        return pltpu.make_async_remote_copy(
            src_ref=residual, dst_ref=residuals.at[row],
            send_sem=residual_send.at[0], recv_sem=residual_recv.at[row],
            device_id=(LAST, 2 * chip), device_id_type=MESH)

    def result_copy(step, to_core):
        return pltpu.make_async_remote_copy(
            src_ref=result.at[mine], dst_ref=result.at[mine],
            send_sem=result_send.at[step, to_core], recv_sem=result_recv.at[mine],
            device_id=(row, 2 * other_chip(step) + to_core), device_id_type=MESH)

    def solved_copy(r):
        return pltpu.make_async_remote_copy(
            src_ref=solved.at[r], dst_ref=result.at[mine],
            send_sem=solved_send.at[r], recv_sem=result_recv.at[mine],
            device_id=(r, 2 * chip + 1), device_id_type=MESH)

    def result_wait(at):
        pltpu.make_async_remote_copy(
            src_ref=solved.at[0], dst_ref=result.at[at],
            send_sem=result_send.at[0, 0], recv_sem=result_recv.at[at],
            device_id=(row, col), device_id_type=MESH).wait_recv()

    @pl.when(side & (row == LAST))
    def _():
        for i in range(max(len(UP), len(DOWN))):
            for piece in DOWN[i:i + 1]:
                pass_on(piece, 1)
            for piece in UP[i:i + 1]:
                pass_on(piece, CHIPS - 1)

    for via, pieces in VIA.items():
        @pl.when(owner & (row == via))
        def _():
            for piece in pieces:
                pass_on(piece, 0)

    @pl.when(reducer)
    def _():
        for k in range(1, CHIPS):
            src = other_chip(k)
            pltpu.make_async_remote_copy(
                src_ref=sums.at[0], dst_ref=parts.at[src],
                send_sem=part_send.at[0], recv_sem=part_recv.at[src],
                device_id=(row, col), device_id_type=MESH).wait_recv()
        value = base[mine]
        for k in range(1, CHIPS):
            value -= parts[other_chip(k)].astype(F32)
        residual[...] = value.astype(BF16)
        residual_copy().start()

    @pl.when(solver)
    def _():
        done = []
        for group in GROUPS:
            for r in group:
                pltpu.make_async_remote_copy(
                    src_ref=residual, dst_ref=residuals.at[r],
                    send_sem=residual_send.at[0], recv_sem=residual_recv.at[r],
                    device_id=(LAST, col), device_id_type=MESH).wait_recv()
                for piece in PIECES:
                    if piece[0] == r:
                        straight_copy(piece).wait_recv()
            blocks = {r: [factor[r, j] if r < LAST else scaled[j] for j in range(r)] for r in group}
            start = {r: dot_t(residuals[r], dinv[r * BS:(r + 1) * BS, :]) for r in group}
            top = group[0]
            if top:
                known = jnp.concatenate(done, 1)
                for r in group:
                    start[r] -= dot_t(known, jnp.concatenate(blocks[r][:top], 1))
            for r in group:
                block = start[r]
                if r - top > 1:
                    block -= dot_t(
                        jnp.concatenate(done[top:r - 1], 1), jnp.concatenate(blocks[r][top:r - 1], 1))
                if r > top:
                    block -= dot_t(done[r - 1], blocks[r][r - 1])
                block = block.astype(BF16)
                done.append(block)
                solved[r] = block
                solved_copy(r).start()

    @pl.when(reducer)
    def _():
        result_wait(mine)
        for step in FAR_FIRST:
            for to_core in (1, 0):
                result_copy(step, to_core).start()
        result_copy(0, 0).start()

    for step in range(1, SOLVERS):
        result_wait(lax.rem(mine + step, SOLVERS))

    @pl.when(jnp.logical_not(reducer))
    def _():
        result_wait(mine)

    out[...] = result[...].reshape(WIDTH, BS)

    for piece in STRAIGHT:
        @pl.when(owner & (row == piece[0]))
        def _():
            straight_copy(piece).wait_send()

    for via, pieces in VIA.items():
        for piece in pieces:
            @pl.when(owner & (row == piece[0]))
            def _():
                first_leg(piece, via).wait_send()

            @pl.when(owner & (row == via))
            def _():
                second_leg(piece, 0).wait_send()

    for piece in UP + DOWN:
        @pl.when(side & (row == piece[0]))
        def _():
            first_leg(piece, LAST).wait_send()

        @pl.when(side & (row == LAST))
        def _():
            second_leg(piece, 1).wait_send()

    @pl.when(first)
    def _():
        give_copy().wait_send()

    @pl.when(core == 1)
    def _():
        for step in (2, 3, 1):
            part_copy(step).wait_send()

        @pl.when(jnp.logical_not(even))
        def _():
            part_copy(0).wait_send()

    @pl.when(reducer)
    def _():
        residual_copy().wait_send()
        for step in FAR_FIRST:
            for to_core in (1, 0):
                result_copy(step, to_core).wait_send()
        result_copy(0, 0).wait_send()

    @pl.when(solver)
    def _():
        for r in range(ROWS):
            solved_copy(r).wait_send()


def on_device(
    rhs, sep_lower, sep_pattern, diag_inverse, child_lower, child_ids, child_count, child_x
):
    dma = pltpu.SemaphoreType.DMA
    found = pl.pallas_call(
        kernel,
        out_shape=pltpu.VMEM((WIDTH, BS), BF16),
        in_specs=[pl.BlockSpec(memory_space=pltpu.HBM)] * 8,
        out_specs=pl.BlockSpec(memory_space=pltpu.VMEM),
        scratch_shapes=[
            pltpu.SMEM((ROWS, ROWS), jnp.int32),
            pltpu.SMEM((1, SLOTS), jnp.int32),
            pltpu.SMEM((1, 1), jnp.int32),
            pltpu.VMEM((BLOCKS + 1, BS, WIDTH), BF16),
            pltpu.VMEM((CHUNKS, BS, SLOTS * BS // CHUNKS), BF16),
            pltpu.VMEM((BS, ROWS * BS), BF16),
            pltpu.VMEM((ROWS * BS, BS), BF16),
            pltpu.VMEM((BS, WIDTH), F32),
            pltpu.VMEM((LAST, BS, BS), BF16),
            pltpu.VMEM((LAST, LAST - 1, BS, BS), BF16),
            pltpu.VMEM((RELAY_BLOCKS, BS, BS), BF16),
            pltpu.VMEM((SOLVERS, PART, BS), F32),
            pltpu.VMEM((SOLVERS, PART, BS), BF16),
            pltpu.VMEM((SOLVERS, PART, BS), BF16),
            pltpu.VMEM((CHIPS, PART, BS), BF16),
            pltpu.VMEM((SOLVERS, PART, BS), F32),
            pltpu.VMEM((PART, BS), BF16),
            pltpu.VMEM((ROWS, PART, BS), BF16),
            pltpu.VMEM((ROWS, PART, BS), BF16),
            pltpu.VMEM((SOLVERS, PART, BS), BF16),
            dma((7 + CHUNKS,)),
            dma((len(PIECES),)),
            dma((len(PIECES),)),
            dma((len(PIECES),)),
            dma((len(PIECES),)),
            dma((1,)),
            dma((1,)),
            dma((SOLVERS,)),
            dma((CHIPS,)),
            dma((1,)),
            dma((ROWS,)),
            dma((ROWS,)),
            dma((CHIPS, 2)),
            dma((SOLVERS,)),
        ],
        compiler_params=pltpu.CompilerParams(
            collective_id=0, has_side_effects=True, vmem_limit_bytes=60 * 2**20
        ),
    )(
        sep_pattern, child_ids, child_count, rhs, sep_lower, diag_inverse, child_lower,
        child_x.reshape(BLOCKS, BS, WIDTH),
    )
    return found.T


def solution(mesh):
    in_specs = (
        P("row", None),
        P("row", None),
        P(),
        P(),
        P("row", "col"),
        P("row", "col"),
        P("row", "col"),
        P("col", None),
    )
    return jax.shard_map(
        on_device, mesh=mesh, in_specs=in_specs, out_specs=P("row", None), check_vma=False
    )
```
